32 devices in a mesh: grp: 4 (over y, x), dom: 8 (over z, core).
Axes of the slice: x: 2, y: 2, z: 4, core: 2. Of those that a mesh axis runs over, the one named last changes fastest.
Arguments:
- features: bfloat16 [98304, 256], P(('grp', 'dom')), may hold values from -6 to 6
- boundary_cache: float32 [8192, 256], P(('grp', 'dom')), may hold values from -6 to 6
- adjacency: bfloat16 [768, 2, 128, 128], P(('grp', 'dom')), may hold values from -0.375 to 0.375
- neighbor: int32 [768, 2], P(('grp', 'dom')), may hold values from 0 to 31
- counts: int32 [768], P(('grp', 'dom')), may hold values from 1 to 2
- wanted: int32 [32, 8], P(('grp', 'dom')), may hold values from 0 to 1
- weight_in: bfloat16 [512, 512], replicated, may hold values from -0.25 to 0.25
- weight_out: bfloat16 [512, 256], replicated, may hold values from -0.25 to 0.25
- cotangent: bfloat16 [98304, 256], P(('grp', 'dom')), may hold values from -6 to 6
Outputs:
- grad_features: bfloat16 [98304, 256], P(('grp', 'dom'))
- grad_weight_in: float32 [512, 512], P('dom')
- grad_weight_out: float32 [512, 256], P('dom')
The draws below stay inside these ranges and needn't reach their ends.
Inputs may be any that keep to these rules, and one draw needn't show every extreme that they name: `neighbor`: A value under 24 names a block of the same partition; a value 24 + q names the boundary block that the partition reads from partition q of its group. Slots from counts[b] on are padding and carry no edges.
All inputs are finite; a program needn't handle non-finite values.
Results may differ from the reference program's by a relative error of at most 0.0054.
Values may be sent and summed in bfloat16 or wider, within the bound.
A program may use at most 128 MiB of HBM per device.

```python
import jax
import jax.numpy as jnp
from jax import lax

F = 256
HID = 512
BLK = 128
S = 2
E = 2
NB_DEV = 24
NODES = 98304
N_GRP = 4
N_DOM = 8


def touch_ends(result, rng, low, high):
    longest = result.shape.index(max(result.shape))
    spots = []
    for shift in (0, 1):
        where = [jax.random.randint(jax.random.fold_in(rng, axis), (), 0, length) for axis, length in enumerate(result.shape)]
        where[longest] = (where[longest] + shift) % result.shape[longest]
        spots.append(tuple(where))
    return result.at[spots[0]].set(low).at[spots[1]].set(high)


def levels(stream_key, extent, split, smallest, top_value):
    factor_of = 1.0
    for axis_at, blocks in split:
        heights = jax.random.uniform(jax.random.fold_in(jax.random.fold_in(stream_key, 6), axis_at), (blocks,), jnp.float32, smallest / len(split), top_value / len(split))
        factor_of = factor_of * jnp.repeat(jnp.exp(heights), extent[axis_at] // blocks).reshape((-1,) + (1,) * (len(extent) - 1 - axis_at))
    return factor_of


def noise(key, shape, scale, limit, pieces=(), held_as=jnp.bfloat16):
    drawn = jax.random.normal(key, shape, jnp.float32) * scale
    if len(pieces) > 0:
        drawn = levels(key, shape, pieces, -0.22, 0.18) * drawn
    return jnp.clip(drawn, min=-limit, max=limit).astype(held_as)


def setup_inputs(seed: int = 0) -> dict:
    arg_keys = jax.random.split(jax.random.key(seed), 10)
    return {
        "features": noise(arg_keys[0], (NODES, F), 1.0, 6.0, ((0, 32),)),
        "boundary_cache": noise(arg_keys[1], (E * BLK * N_GRP * N_DOM, F), 1.0, 6.0, ((0, 32),), jnp.float32),
        "adjacency": noise(arg_keys[2], (NB_DEV * N_GRP * N_DOM, S, BLK, BLK), (BLK * S) ** -0.5, 0.375, ((0, 32),)),
        "neighbor": touch_ends(jax.random.randint(arg_keys[3], (NB_DEV * N_GRP * N_DOM, S), 0, NB_DEV + N_DOM), jax.random.fold_in(arg_keys[3], 1), 0, (NB_DEV + N_DOM) - 1).astype(jnp.int32),
        "counts": touch_ends(jax.random.randint(arg_keys[4], (NB_DEV * N_GRP * N_DOM,), 1, S + 1), jax.random.fold_in(arg_keys[4], 1), 1, S).astype(jnp.int32),
        "wanted": touch_ends(jax.random.randint(arg_keys[5], (N_GRP * N_DOM, N_DOM), 0, E), jax.random.fold_in(arg_keys[5], 1), 0, E - 1).astype(jnp.int32),
        "weight_in": noise(arg_keys[6], (2 * F, HID), (2 * F) ** -0.5, 0.25),
        "weight_out": noise(arg_keys[7], (HID, F), HID ** -0.5, 0.25),
        "cotangent": noise(arg_keys[8], (NODES, F), 1.0, 6.0, ((0, 32),)),
    }


def partition_grads(features_p, adjacency_p, neighbor_p, counts_p, wanted_p, cotangent_p, group_cache, weight_in, weight_out):
    block_rows = adjacency_p.shape[2]
    nblocks = adjacency_p.shape[0]
    slot_total = adjacency_p.shape[1]
    channels = features_p.shape[1]
    boundary = jnp.take_along_axis(group_cache, wanted_p[:, None, None, None], axis=1)[:, 0]
    owned = features_p.reshape(nblocks, block_rows, channels)
    sources = jnp.concatenate([owned, boundary], 0)
    active = jnp.arange(slot_total)[None, :] < counts_p[:, None]
    chosen = sources[neighbor_p]
    chosen = jnp.where(active[:, :, None, None], chosen, jnp.zeros_like(chosen))
    aggregate = jnp.einsum("bsij,bsjf->bif", adjacency_p.astype(jnp.float32), chosen.astype(jnp.float32))
    aggregate = aggregate.astype(jnp.bfloat16).reshape(nblocks * block_rows, channels)
    joined = jnp.concatenate([aggregate, features_p], 1)
    preact = jnp.dot(joined, weight_in, preferred_element_type=jnp.float32)
    gating = jax.nn.sigmoid(preact)
    hidden = (preact * gating).astype(jnp.bfloat16)
    grad_hidden = jnp.dot(cotangent_p, weight_out.T, preferred_element_type=jnp.float32)
    grad_preact = (grad_hidden * gating * (1.0 + preact * (1.0 - gating))).astype(jnp.bfloat16)
    grad_joined = jnp.dot(grad_preact, weight_in.T, preferred_element_type=jnp.float32)
    grad_aggregate = grad_joined[:, :channels].astype(jnp.bfloat16).reshape(nblocks, block_rows, channels)
    backward = jnp.einsum("bsji,bjf->bsif", adjacency_p.astype(jnp.float32), grad_aggregate.astype(jnp.float32))
    local_hit = active & (neighbor_p < nblocks)
    routing = (neighbor_p[None, :, :] == jnp.arange(nblocks)[:, None, None]) & local_hit[None]
    spread = jnp.einsum("cbs,bsif->cif", routing.astype(jnp.float32), backward, precision=lax.Precision.HIGHEST)
    grad_features = (grad_joined[:, channels:] + spread.reshape(nblocks * block_rows, channels)).astype(jnp.bfloat16)
    term_in = jnp.dot(joined.T.astype(jnp.float32), grad_preact.astype(jnp.float32), precision=lax.Precision.HIGHEST)
    term_out = jnp.dot(hidden.T.astype(jnp.float32), cotangent_p.astype(jnp.float32), precision=lax.Precision.HIGHEST)
    return grad_features, term_in, term_out


def reference(features, boundary_cache, adjacency, neighbor, counts, wanted, weight_in, weight_out, cotangent):
    parts = N_GRP * N_DOM
    cache_copy = boundary_cache.astype(jnp.bfloat16).reshape(N_GRP, N_DOM, E, BLK, F)
    features_all = features.reshape(parts, NB_DEV * BLK, F)
    cotangent_all = cotangent.reshape(parts, NB_DEV * BLK, F)
    adjacency_all = adjacency.reshape(parts, NB_DEV, S, BLK, BLK)
    neighbor_all = neighbor.reshape(parts, NB_DEV, S)
    counts_all = counts.reshape(parts, NB_DEV)
    groups = (jnp.arange(parts) // N_DOM).astype(jnp.int32)

    def step(carry, inputs):
        features_p, adjacency_p, neighbor_p, counts_p, wanted_p, cotangent_p, group = inputs
        group_cache = lax.dynamic_index_in_dim(cache_copy, group, 0, keepdims=False)
        grad_features, term_in, term_out = partition_grads(features_p, adjacency_p, neighbor_p, counts_p, wanted_p, cotangent_p, group_cache, weight_in, weight_out)
        return (carry[0] + term_in, carry[1] + term_out), grad_features

    start_sums = (jnp.zeros((2 * F, HID), jnp.float32), jnp.zeros((HID, F), jnp.float32))
    sums, grad_features = lax.scan(step, start_sums, (features_all, adjacency_all, neighbor_all, counts_all, wanted, cotangent_all, groups))
    loss_scale = NODES ** -0.5
    return grad_features.reshape(NODES, F), sums[0] * loss_scale, sums[1] * loss_scale
```

```python
import functools
import math

import jax
import jax.numpy as jnp
from jax import lax
from jax.experimental import pallas as pl
from jax.experimental.pallas import tpu as pltpu
from jax.sharding import PartitionSpec as P

F32, BF16 = jnp.float32, jnp.bfloat16
TILE = 512
NT_DIMS = (((1,), (1,)), ((), ()))


def mm(a, b):
    return jnp.dot(a, b, preferred_element_type=F32)


def mm_nt(a, b):
    return lax.dot_general(a, b, NT_DIMS, preferred_element_type=F32)


def layer_kernel(
    n_grp, n_dom,
    nbr, cnt, wnt, feat_h, cache_h, adj_h, win_h, wout_h, cot_h,
    base_h, gagg_h, gw_h,
    src, cache, adj, win, wout, cot, win_t, pre2, gh, gps, acc_in, acc_out,
    base, gagg, own1, sb1, rb1, chip, sb2, rb2, sb3, rb3, gat4,
    load_sem, out_sem, b_send, b_recv, s1, r1, s2, r2, s3, r3, s4, r4,
):
    nb, slots, blk, _ = adj.shape
    exports = cache.shape[0] // blk
    line = n_dom // 2
    tiles = cot.shape[0]
    per = TILE // blk
    ch = cot.shape[2]
    hid_n = wout.shape[0]
    rows = rb1.shape[1]
    zero_block = nb + n_dom * exports

    g = lax.axis_index("grp")
    d = lax.axis_index("dom")
    z, c = d // 2, lax.rem(d, 2)
    pair = z * 2 + (1 - c)

    def load(i, a, b):
        return pltpu.make_async_copy(a, b, load_sem.at[i])

    loads = [
        load(0, cache_h, cache),
        load(1, wout_h, wout),
        load(2, cot_h, cot),
        load(3, win_h, win),
        load(4, feat_h, src.at[pl.ds(0, nb)]),
        load(5, adj_h, adj),
    ]
    for item in loads:
        item.start()

    barrier = pltpu.get_barrier_semaphore()
    peers = [(g, pair)]
    peers += [(g, 2 * lax.rem(z + k, line) + c) for k in range(1, line)]
    peers += [(lax.rem(g + k, n_grp), d) for k in range(1, n_grp)]
    for peer in peers:
        pl.semaphore_signal(barrier, inc=1, device_id=peer, device_id_type=pl.DeviceIdType.MESH)

    loads[0].wait()
    src[pl.ds(nb + d * exports, exports)] = cache[...].astype(BF16).reshape(exports, blk, ch)
    pl.semaphore_wait(barrier, len(peers))

    def remote(a, b, send, recv, where):
        return pltpu.make_async_remote_copy(
            src_ref=a, dst_ref=b, send_sem=send, recv_sem=recv,
            device_id=where, device_id_type=pl.DeviceIdType.MESH,
        )

    def spread(q, way):
        part = src.at[pl.ds(nb + q * exports, exports)]
        to = (d + 2, d - 2, pair)[way]
        return remote(part, part, b_send.at[q, way], b_recv.at[q], (g, to))

    not_last, not_first = z < line - 1, z > 0
    pl.when(not_last)(lambda: spread(d, 0).start())
    pl.when(not_first)(lambda: spread(d, 1).start())
    spread(d, 2).start()

    for item in loads[1:5]:
        item.wait()
    win_t[...] = win[...].astype(F32).T.astype(BF16)
    src[zero_block] = jnp.zeros((blk, ch), BF16)

    def early(i, carry):
        gh[i] = mm_nt(wout[...], cot[i])
        own = src[pl.ds(i * per, per)].reshape(TILE, ch)
        pre2[i] = mm_nt(win_t[:, ch:], own)
        return carry

    done = 0
    for k in range(1, line):
        upto = tiles * k // (line - 1)
        lax.fori_loop(done, upto, early, 0)
        done = upto

        @pl.when(z - k >= 0)
        def _():
            q = d - 2 * k
            spread(q, 0).wait_recv()
            pl.when(not_last)(lambda: spread(q, 0).start())
            spread(q, 2).start()

        @pl.when(z + k < line)
        def _():
            q = d + 2 * k
            spread(q, 1).wait_recv()
            pl.when(not_first)(lambda: spread(q, 1).start())
            spread(q, 2).start()

    acc_in[...] = jnp.zeros_like(acc_in)
    acc_out[...] = jnp.zeros_like(acc_out)
    loads[5].wait()
    for zz in range(line):
        spread(2 * zz + 1 - c, 2).wait_recv()

    def source(b, s):
        n = nbr[b, s]
        far = jnp.maximum(n - nb, 0)
        n = jnp.where(n < nb, n, nb + far * exports + wnt[0, far])
        return src[jnp.where(s < cnt[b], n, zero_block)]

    def main(i, carry):
        parts = []
        for k in range(per):
            b = i * per + k
            left = jnp.concatenate([adj[b, s] for s in range(slots)], axis=1)
            right = jnp.concatenate([source(b, s) for s in range(slots)], axis=0)
            parts.append(mm(left, right).astype(BF16))
        agg = jnp.concatenate(parts, axis=0)
        pre = pre2[i] + mm_nt(win_t[:, :ch], agg)
        sg = 0.5 + 0.5 * jnp.tanh(0.5 * pre)
        h = pre * sg
        gp = (gh[i] * (sg + h * (1.0 - sg))).astype(BF16)
        gps[i] = gp
        own = src[pl.ds(i * per, per)].reshape(TILE, ch)
        for m, part in enumerate((agg, own)):
            term = mm(gp, part)
            for j in range(ch // (2 * rows)):
                at = m * (ch // (2 * rows)) + j
                acc_in[at] += term[:, j * 2 * rows : (j + 1) * 2 * rows]
        acc_out[...] += mm(h.astype(BF16), cot[i]).reshape(acc_out.shape)
        return carry

    lax.fori_loop(0, tiles, main, 0)

    def late(i, carry):
        gj = mm(win[...], gps[i]).astype(BF16)
        for k in range(per):
            cols = slice(k * blk, (k + 1) * blk)
            gagg[i * per + k] = gj[:ch, cols]
            base[i * per + k] = gj[ch:, cols]
        return carry

    order = [lax.rem(z + k, line) for k in range(1, line + 1)]

    def step1(zz):
        return remote(sb1.at[zz, 1 - c], rb1.at[zz], s1.at[zz], r1.at[zz], (g, pair))

    for zz in order:
        whole = jnp.concatenate([acc_in[zz].T, acc_out[zz]], axis=1)
        whole = whole.reshape(2, rows, whole.shape[1])
        own1[zz] = whole
        sb1[zz] = whole.astype(BF16)
        step1(zz).start()

    def step2(zz, k):
        to = lax.rem(g + k, n_grp)
        return remote(
            sb2.at[zz, to], rb2.at[k - 1, zz], s2.at[k - 1, zz], r2.at[k - 1, zz], (to, d)
        )

    for zz in order:
        step1(zz).wait_recv()
        both = (own1[zz, c] + rb1[zz].astype(F32)).reshape(chip.shape[1:])
        chip[zz] = both
        sb2[zz] = both.astype(BF16)
        for k in range(1, n_grp):
            step2(zz, k).start()

    lax.fori_loop(0, tiles, late, 0)
    stores = [
        pltpu.make_async_copy(base, base_h, out_sem.at[0]),
        pltpu.make_async_copy(gagg, gagg_h, out_sem.at[1]),
    ]
    for item in stores:
        item.start()

    def step3(k):
        to = lax.rem(z + k, line)
        return remote(sb3.at[k - 1], rb3.at[k - 1], s3.at[k - 1], r3.at[k - 1], (g, 2 * to + c))

    total = None
    for k, zz in enumerate(order, 1):
        total = chip[zz, g]
        for j in range(1, n_grp):
            step2(zz, j).wait_recv()
            total += rb2[j - 1, zz].astype(F32)
        if k < line:
            sb3[k - 1] = total.astype(BF16)
            step3(k).start()
    for k in range(1, line):
        step3(k).wait_recv()
        total += rb3[k - 1].astype(F32)

    def step4(k):
        to = lax.rem(g + k, n_grp)
        return remote(gat4.at[g], gat4.at[g], s4.at[k - 1], r4.at[k - 1], (to, d))

    def arrive4(k):
        there = gat4.at[lax.rem(g - k + n_grp, n_grp)]
        return remote(there, there, s4.at[k - 1], r4.at[k - 1], (lax.rem(g + k, n_grp), d))

    gat4[g] = total.astype(BF16)
    for k in range(1, n_grp):
        step4(k).start()
    for k in range(1, n_grp):
        arrive4(k).wait_recv()
    last = pltpu.make_async_copy(gat4, gw_h, out_sem.at[2])
    last.start()

    pl.when(not_last)(lambda: spread(d, 0).wait_send())
    pl.when(not_first)(lambda: spread(d, 1).wait_send())
    spread(d, 2).wait_send()
    for k in range(1, line):

        @pl.when(z - k >= 0)
        def _():
            q = d - 2 * k
            pl.when(not_last)(lambda: spread(q, 0).wait_send())
            spread(q, 2).wait_send()

        @pl.when(z + k < line)
        def _():
            q = d + 2 * k
            pl.when(not_first)(lambda: spread(q, 1).wait_send())
            spread(q, 2).wait_send()

    for zz in order:
        step1(zz).wait_send()
        for k in range(1, n_grp):
            step2(zz, k).wait_send()
    for k in range(1, line):
        step3(k).wait_send()
    for k in range(1, n_grp):
        step4(k).wait_send()
    for item in stores:
        item.wait()
    last.wait()


def finish_kernel(scale, nbr, cnt, adj, base, gagg, gw, out, gw_in, gw_out, acc):
    nb, slots, blk, _ = adj.shape
    hid_n = gw_in.shape[1]
    value = gw[...].astype(F32) * scale
    gw_in[...] = value[:, :hid_n]
    gw_out[...] = value[:, hid_n:]
    acc[pl.ds(0, nb)] = base[...].astype(F32)

    def body(b, carry):
        term = mm(gagg[b], jnp.concatenate([adj[b, s] for s in range(slots)], axis=1))
        for s in range(slots):
            n = nbr[b, s]
            live = jnp.logical_and(s < cnt[b], n < nb)
            acc[jnp.where(live, n, nb)] += term[:, s * blk : (s + 1) * blk]
        return carry

    lax.fori_loop(0, nb, body, 0)

    def write(b, carry):
        out[b] = acc[b].T.astype(BF16)
        return carry

    lax.fori_loop(0, nb, write, 0)


def fast_local(
    features, boundary_cache, adjacency, neighbor, counts, wanted, weight_in, weight_out, cotangent
):
    nb, slots, blk, _ = adjacency.shape
    node_rows, ch = features.shape
    hid_n = weight_out.shape[0]
    n_grp, n_dom = lax.axis_size("grp"), lax.axis_size("dom")
    line = n_dom // 2
    tiles = node_rows // TILE
    exports = boundary_cache.shape[0] // blk
    rows = hid_n // n_dom
    wide = hid_n + ch
    share = rows // n_grp
    any_spec = pl.BlockSpec(memory_space=pl.ANY)
    smem = pl.BlockSpec(memory_space=pltpu.SMEM)
    vmem = pl.BlockSpec(memory_space=pltpu.VMEM)
    dma = pltpu.SemaphoreType.DMA
    V = pltpu.VMEM
    nodes = node_rows
    cost = pl.CostEstimate(
        flops=2 * nodes * hid_n * (7 * ch), bytes_accessed=8 * nodes * ch,
        transcendentals=nodes * hid_n,
    )
    base, gagg, gw = pl.pallas_call(
        functools.partial(layer_kernel, n_grp, n_dom),
        out_shape=(
            jax.ShapeDtypeStruct((nb, ch, blk), BF16),
            jax.ShapeDtypeStruct((nb, ch, blk), BF16),
            jax.ShapeDtypeStruct((n_grp, share, wide), BF16),
        ),
        in_specs=[smem] * 3 + [any_spec] * 6,
        out_specs=(any_spec,) * 3,
        scratch_shapes=[
            V((nb + n_dom * exports + 1, blk, ch), BF16),
            V(boundary_cache.shape, F32),
            V(adjacency.shape, BF16),
            V(weight_in.shape, BF16),
            V(weight_out.shape, BF16),
            V((tiles, TILE, ch), BF16),
            V((hid_n, 2 * ch), BF16),
            V((tiles, hid_n, TILE), F32),
            V((tiles, hid_n, TILE), F32),
            V((tiles, hid_n, TILE), BF16),
            V((line, hid_n, 2 * rows), F32),
            V((line, 2 * rows, ch), F32),
            V((nb, ch, blk), BF16),
            V((nb, ch, blk), BF16),
            V((line, 2, rows, wide), F32),
            V((line, 2, rows, wide), BF16),
            V((line, rows, wide), BF16),
            V((line, n_grp, share, wide), F32),
            V((line, n_grp, share, wide), BF16),
            V((n_grp - 1, line, share, wide), BF16),
            V((line - 1, share, wide), BF16),
            V((line - 1, share, wide), BF16),
            V((n_grp, share, wide), BF16),
            dma((6,)), dma((3,)),
            dma((n_dom, 3)), dma((n_dom,)),
            dma((line,)), dma((line,)),
            dma((n_grp - 1, line)), dma((n_grp - 1, line)),
            dma((line - 1,)), dma((line - 1,)),
            dma((n_grp - 1,)), dma((n_grp - 1,)),
        ],
        compiler_params=pltpu.CompilerParams(
            collective_id=0, has_side_effects=True, vmem_limit_bytes=56 * 2**20
        ),
        cost_estimate=cost,
    )(
        neighbor, counts, wanted, features.reshape(nb, blk, ch), boundary_cache, adjacency,
        weight_in, weight_out, cotangent.reshape(tiles, TILE, ch),
    )
    node_total = node_rows * n_grp * n_dom
    grad_features, gw_in, gw_out = pl.pallas_call(
        functools.partial(finish_kernel, 1.0 / math.sqrt(node_total)),
        out_shape=(
            jax.ShapeDtypeStruct((nb, blk, ch), BF16),
            jax.ShapeDtypeStruct((rows, hid_n), F32),
            jax.ShapeDtypeStruct((rows, ch), F32),
        ),
        in_specs=[smem] * 2 + [vmem] * 4,
        out_specs=(vmem,) * 3,
        scratch_shapes=[V((nb + 1, ch, blk), F32)],
        compiler_params=pltpu.CompilerParams(vmem_limit_bytes=32 * 2**20),
    )(neighbor, counts, adjacency, base, gagg, gw.reshape(rows, wide))
    return grad_features.reshape(node_rows, ch), gw_in, gw_out


def local(
    features, boundary_cache, adjacency, neighbor, counts, wanted, weight_in, weight_out, cotangent
):
    nblocks = adjacency.shape[0]
    slot_total = adjacency.shape[1]
    block_rows = adjacency.shape[2]
    channels = features.shape[1]
    node_rows = nblocks * block_rows
    partners = lax.axis_size("dom")
    cache_copy = boundary_cache.astype(jnp.bfloat16)
    exported = cache_copy.reshape(-1, block_rows, channels)
    export_total = exported.shape[0]
    exported_all = lax.all_gather(cache_copy, "dom", axis=0, tiled=True).reshape(
        partners, export_total, block_rows, channels
    )
    selected = wanted[0]
    boundary = exported_all[:, 0]
    boundary = jnp.where((selected == 1)[:, None, None], exported_all[:, 1], boundary)
    owned = features.reshape(nblocks, block_rows, channels)
    sources = jnp.concatenate([owned, boundary], 0)
    active = jnp.arange(slot_total)[None, :] < counts[:, None]
    chosen = sources[neighbor]
    chosen = jnp.where(active[:, :, None, None], chosen, jnp.zeros_like(chosen))
    aggregate = jnp.einsum("bsij,bsjf->bif", adjacency, chosen, preferred_element_type=jnp.float32)
    aggregate = aggregate.astype(jnp.bfloat16).reshape(node_rows, channels)
    joined = jnp.concatenate([aggregate, features], 1)
    preact = jnp.dot(joined, weight_in, preferred_element_type=jnp.float32)
    gating = jax.nn.sigmoid(preact)
    hidden = (preact * gating).astype(jnp.bfloat16)
    grad_hidden = jnp.einsum("nf,hf->nh", cotangent, weight_out, preferred_element_type=jnp.float32)
    grad_preact = (grad_hidden * gating * (1.0 + preact * (1.0 - gating))).astype(jnp.bfloat16)
    grad_joined = jnp.einsum(
        "nh,ch->nc", grad_preact, weight_in, preferred_element_type=jnp.float32
    )
    grad_aggregate = (
        grad_joined[:, :channels].astype(jnp.bfloat16).reshape(nblocks, block_rows, channels)
    )
    backward = jnp.einsum(
        "bsji,bjf->bsif", adjacency, grad_aggregate, preferred_element_type=jnp.float32
    )
    local_hit = active & (neighbor < nblocks)
    routing = (neighbor[None, :, :] == jnp.arange(nblocks)[:, None, None]) & local_hit[None]
    spread = jnp.einsum(
        "cbs,bsif->cif", routing.astype(jnp.float32), backward, precision=lax.Precision.HIGHEST
    )
    grad_features = (grad_joined[:, channels:] + spread.reshape(node_rows, channels)).astype(
        jnp.bfloat16
    )
    node_total = node_rows * lax.axis_size("grp") * partners
    loss_scale = 1.0 / math.sqrt(node_total)
    rows_in = weight_in.shape[0] // partners
    rows_out = weight_out.shape[0] // partners
    summed = lax.psum(
        (
            jnp.einsum("nc,nh->ch", joined, grad_preact, preferred_element_type=jnp.float32)
            * loss_scale,
            jnp.einsum("nh,nf->hf", hidden, cotangent, preferred_element_type=jnp.float32)
            * loss_scale,
        ),
        ("grp", "dom"),
    )
    position = lax.axis_index("dom")
    grad_weight_in = lax.dynamic_slice_in_dim(summed[0], position * rows_in, rows_in, 0)
    grad_weight_out = lax.dynamic_slice_in_dim(summed[1], position * rows_out, rows_out, 0)
    return (grad_features, grad_weight_in, grad_weight_out)


def solution(mesh):
    in_specs = (
        P(("grp", "dom"), None),
        P(("grp", "dom"), None),
        P(("grp", "dom"), None, None, None),
        P(("grp", "dom"), None),
        P(("grp", "dom")),
        P(("grp", "dom"), None),
        P(),
        P(),
        P(("grp", "dom"), None),
    )
    out_specs = (P(("grp", "dom"), None), P("dom", None), P("dom", None))
    n_grp, n_dom = mesh.shape["grp"], mesh.shape["dom"]

    def program(*args):
        rows = args[7].shape[0] // n_dom
        nodes = args[0].shape[0] // (n_grp * n_dom)
        fits = rows % (16 * n_grp) == 0 and (2 * rows) % 128 == 0 and nodes % TILE == 0
        body = fast_local if fits else local
        return sharded(body)(*args)

    def sharded(body):
        return jax.shard_map(
            body, mesh=mesh, in_specs=in_specs, out_specs=out_specs, check_vma=False
        )

    return program
```

```python
import functools
import math

import jax
import jax.numpy as jnp
import numpy as np
from jax import lax
from jax.experimental import pallas as pl
from jax.experimental.pallas import tpu as pltpu
from jax.sharding import PartitionSpec as P

F32, BF16 = jnp.float32, jnp.bfloat16
TILE = 512
NT_DIMS = (((1,), (1,)), ((), ()))


def mm(a, b):
    return jnp.dot(a, b, preferred_element_type=F32)


def mm_nt(a, b):
    return lax.dot_general(a, b, NT_DIMS, preferred_element_type=F32)


def layer_kernel(
    n_grp, n_dom,
    nbr, cnt, prev, last_of, wnt, feat_h, cache_h, adj_h, win_h, wout_h, cot_h,
    out_h, gw_in_h, gw_out_h,
    src, cache, adj, win, wout, cot, win_t, pre2, gh, gps, acc_in, acc_out,
    base, terms, out, own1, sb1, rb1, chip, sb2, rb2, sb3, rb3, gat4,
    load_sem, out_sem, b_send, b_recv, s1, r1, s2, r2, s3, r3, s4, r4,
):
    nb, slots, blk, _ = adj.shape
    exports = cache.shape[0] // blk
    line = n_dom // 2
    tiles = cot.shape[0]
    per = TILE // blk
    ch = cot.shape[2]
    hid_n = wout.shape[0]
    rows = rb1.shape[1]
    none = nb + n_dom * exports

    g = lax.axis_index("grp")
    d = lax.axis_index("dom")
    z, c = d // 2, lax.rem(d, 2)
    pair = z * 2 + (1 - c)

    def load(i, a, b):
        return pltpu.make_async_copy(a, b, load_sem.at[i])

    loads = [
        load(0, cache_h, cache),
        load(1, wout_h, wout),
        load(2, cot_h, cot),
        load(3, win_h, win),
        load(4, feat_h, src.at[pl.ds(0, nb)]),
        load(5, adj_h, adj),
    ]
    for item in loads:
        item.start()

    barrier = pltpu.get_barrier_semaphore()
    peers = [(g, pair)]
    peers += [(g, 2 * lax.rem(z + k, line) + c) for k in range(1, line)]
    peers += [(lax.rem(g + k, n_grp), d) for k in range(1, n_grp)]
    for peer in peers:
        pl.semaphore_signal(barrier, inc=1, device_id=peer, device_id_type=pl.DeviceIdType.MESH)

    loads[0].wait()
    src[pl.ds(nb + d * exports, exports)] = cache[...].astype(BF16).reshape(exports, blk, ch)
    pl.semaphore_wait(barrier, len(peers))

    def remote(a, b, send, recv, where):
        return pltpu.make_async_remote_copy(
            src_ref=a, dst_ref=b, send_sem=send, recv_sem=recv,
            device_id=where, device_id_type=pl.DeviceIdType.MESH,
        )

    def spread(q, e, way):
        part = src.at[nb + q * exports + e]
        to = (d + 2, d - 2, pair)[way]
        return remote(part, part, b_send.at[q, e, way], b_recv.at[q, e], (g, to))

    not_last, not_first = z < line - 1, z > 0
    for e in range(exports):
        pl.when(not_last)(lambda: spread(d, e, 0).start())
        pl.when(not_first)(lambda: spread(d, e, 1).start())
    for e in range(exports):
        spread(d, e, 2).start()

    for item in loads[1:5]:
        item.wait()
    win_t[...] = win[...].astype(F32).T.astype(BF16)
    src[pl.ds(none, exports)] = jnp.zeros((exports, blk, ch), BF16)
    terms[0] = jnp.zeros((ch, blk), F32)

    def early(i, carry):
        gh[i] = mm_nt(wout[...], cot[i])
        own = src[pl.ds(i * per, per)].reshape(TILE, ch)
        pre2[i] = mm_nt(win_t[:, ch:], own)
        return carry

    done = 0
    for k in range(1, line):
        upto = tiles * k // (line - 1)
        lax.fori_loop(done, upto, early, 0)
        done = upto

        @pl.when(z - k >= 0)
        def _():
            for e in range(exports):
                spread(d - 2 * k, e, 0).wait_recv()
                pl.when(not_last)(lambda: spread(d - 2 * k, e, 0).start())
                spread(d - 2 * k, e, 2).start()

        @pl.when(z + k < line)
        def _():
            for e in range(exports):
                spread(d + 2 * k, e, 1).wait_recv()
                pl.when(not_first)(lambda: spread(d + 2 * k, e, 1).start())
                spread(d + 2 * k, e, 2).start()

    acc_in[...] = jnp.zeros_like(acc_in)
    acc_out[...] = jnp.zeros_like(acc_out)
    loads[5].wait()
    for zz in range(line):
        for e in range(exports):
            spread(2 * zz + 1 - c, e, 2).wait_recv()

    def source(b, s):
        n = jnp.where(s < cnt[b], nbr[s, b], nb + n_dom)
        far = jnp.maximum(n - nb, 0)
        pick = wnt[0, jnp.minimum(far, n_dom - 1)]
        return src[jnp.where(n < nb, n, nb + far * exports + pick)]

    def main(i, carry):
        parts = []
        for k in range(per):
            b = i * per + k
            left = jnp.concatenate([adj[b, s] for s in range(slots)], axis=1)
            right = jnp.concatenate([source(b, s) for s in range(slots)], axis=0)
            parts.append(mm(left, right).astype(BF16))
        agg = jnp.concatenate(parts, axis=0)
        pre = pre2[i] + mm_nt(win_t[:, :ch], agg)
        sg = 0.5 + 0.5 * jnp.tanh(0.5 * pre)
        h = pre * sg
        gp = (gh[i] * (sg + h * (1.0 - sg))).astype(BF16)
        gps[i] = gp
        own = src[pl.ds(i * per, per)].reshape(TILE, ch)
        for m, part in enumerate((agg, own)):
            term = mm(gp, part)
            for j in range(ch // (2 * rows)):
                at = m * (ch // (2 * rows)) + j
                acc_in[at] += term[:, j * 2 * rows : (j + 1) * 2 * rows]
        acc_out[...] += mm(h.astype(BF16), cot[i]).reshape(acc_out.shape)
        return carry

    lax.fori_loop(0, tiles, main, 0)

    def late(i, carry):
        gj = mm(win[...], gps[i])
        gagg = gj[:ch].astype(BF16)
        for k in range(per):
            b = i * per + k
            cols = slice(k * blk, (k + 1) * blk)
            base[b] = gj[ch:, cols]
            both = mm(gagg[:, cols], jnp.concatenate([adj[b, s] for s in range(slots)], axis=1))
            for s in range(slots):
                terms[1 + b * slots + s] = both[:, s * blk : (s + 1) * blk]
        return carry

    def chain(b, carry):
        for s in range(slots):
            terms[1 + b * slots + s] += terms[prev[s, b]]
        return carry

    def write(b, carry):
        out[b] = (base[b] + terms[last_of[b]]).T.astype(BF16)
        return carry

    order = [lax.rem(z + k, line) for k in range(1, line + 1)]

    def step1(zz):
        return remote(sb1.at[zz, 1 - c], rb1.at[zz], s1.at[zz], r1.at[zz], (g, pair))

    for zz in order:
        whole = jnp.concatenate([acc_in[zz].T, acc_out[zz]], axis=1)
        whole = whole.reshape(2, rows, whole.shape[1])
        own1[zz] = whole
        sb1[zz] = whole.astype(BF16)
        step1(zz).start()

    def step2(zz, k):
        to = lax.rem(g + k, n_grp)
        return remote(
            sb2.at[zz, to], rb2.at[k - 1, zz], s2.at[k - 1, zz], r2.at[k - 1, zz], (to, d)
        )

    for zz in order:
        step1(zz).wait_recv()
        both = (own1[zz, c] + rb1[zz].astype(F32)).reshape(chip.shape[1:])
        chip[zz] = both
        sb2[zz] = both.astype(BF16)
        for k in range(1, n_grp):
            step2(zz, k).start()

    lax.fori_loop(0, tiles, late, 0)
    def step3(k):
        to = lax.rem(z + k, line)
        return remote(sb3.at[k - 1], rb3.at[k - 1], s3.at[k - 1], r3.at[k - 1], (g, 2 * to + c))

    total = None
    for k, zz in enumerate(order, 1):
        total = chip[zz, g]
        for j in range(1, n_grp):
            step2(zz, j).wait_recv()
            total += rb2[j - 1, zz].astype(F32)
        if k < line:
            sb3[k - 1] = total.astype(BF16)
            step3(k).start()
    lax.fori_loop(0, nb, chain, 0)
    for k in range(1, line):
        step3(k).wait_recv()
        total += rb3[k - 1].astype(F32)

    def step4(k):
        to = lax.rem(g + k, n_grp)
        return remote(gat4.at[g], gat4.at[g], s4.at[k - 1], r4.at[k - 1], (to, d))

    def arrive4(k):
        there = gat4.at[lax.rem(g - k + n_grp, n_grp)]
        return remote(there, there, s4.at[k - 1], r4.at[k - 1], (lax.rem(g + k, n_grp), d))

    gat4[g] = total.astype(BF16)
    for k in range(1, n_grp):
        step4(k).start()
    lax.fori_loop(0, nb, write, 0)
    store = pltpu.make_async_copy(out, out_h, out_sem.at[0])
    store.start()
    for k in range(1, n_grp):
        arrive4(k).wait_recv()
    last = [
        pltpu.make_async_copy(gat4.at[:, :, pl.ds(0, hid_n)], gw_in_h, out_sem.at[1]),
        pltpu.make_async_copy(gat4.at[:, :, pl.ds(hid_n, ch)], gw_out_h, out_sem.at[2]),
    ]
    for item in last:
        item.start()

    for e in range(exports):
        pl.when(not_last)(lambda: spread(d, e, 0).wait_send())
        pl.when(not_first)(lambda: spread(d, e, 1).wait_send())
        spread(d, e, 2).wait_send()
    for k in range(1, line):

        @pl.when(z - k >= 0)
        def _():
            for e in range(exports):
                pl.when(not_last)(lambda: spread(d - 2 * k, e, 0).wait_send())
                spread(d - 2 * k, e, 2).wait_send()

        @pl.when(z + k < line)
        def _():
            for e in range(exports):
                pl.when(not_first)(lambda: spread(d + 2 * k, e, 1).wait_send())
                spread(d + 2 * k, e, 2).wait_send()

    for zz in order:
        step1(zz).wait_send()
        for k in range(1, n_grp):
            step2(zz, k).wait_send()
    for k in range(1, line):
        step3(k).wait_send()
    for k in range(1, n_grp):
        step4(k).wait_send()
    store.wait()
    for item in last:
        item.wait()


def chains(targets, counts, nb):
    slots = targets.shape[0]
    live = jnp.arange(slots)[:, None] < counts[None, :]
    key = jnp.where(live, targets, -1)
    place = 1 + np.arange(nb)[None, :] * slots + np.arange(slots)[:, None]
    place = jnp.asarray(place.astype(np.int32))
    same = key[:, :, None, None] == key[None, None]
    same &= place[None, None] < place[:, :, None, None]
    prev = jnp.max(jnp.where(same, place[None, None], 0), axis=(2, 3))
    mine = key[None] == jnp.arange(nb)[:, None, None]
    return prev, jnp.max(jnp.where(mine, place[None], 0), axis=(1, 2))


def fast_local(
    features, boundary_cache, adjacency, neighbor, counts, wanted, weight_in, weight_out, cotangent
):
    nb, slots, blk, _ = adjacency.shape
    node_rows, ch = features.shape
    hid_n = weight_out.shape[0]
    n_grp, n_dom = lax.axis_size("grp"), lax.axis_size("dom")
    line = n_dom // 2
    tiles = node_rows // TILE
    exports = boundary_cache.shape[0] // blk
    rows = hid_n // n_dom
    wide = hid_n + ch
    share = rows // n_grp
    any_spec = pl.BlockSpec(memory_space=pl.ANY)
    smem = pl.BlockSpec(memory_space=pltpu.SMEM)
    dma = pltpu.SemaphoreType.DMA
    V = pltpu.VMEM
    nodes = node_rows
    cost = pl.CostEstimate(
        flops=2 * nodes * hid_n * (7 * ch), bytes_accessed=8 * nodes * ch,
        transcendentals=nodes * hid_n,
    )
    targets = neighbor.T
    prev, last_of = chains(targets, counts, nb)
    out, gw_in, gw_out = pl.pallas_call(
        functools.partial(layer_kernel, n_grp, n_dom),
        out_shape=(
            jax.ShapeDtypeStruct((nb, blk, ch), BF16),
            jax.ShapeDtypeStruct((n_grp, share, hid_n), BF16),
            jax.ShapeDtypeStruct((n_grp, share, ch), BF16),
        ),
        in_specs=[smem] * 5 + [any_spec] * 6,
        out_specs=(any_spec,) * 3,
        scratch_shapes=[
            V((nb + (n_dom + 1) * exports, blk, ch), BF16),
            V(boundary_cache.shape, F32),
            V(adjacency.shape, BF16),
            V(weight_in.shape, BF16),
            V(weight_out.shape, BF16),
            V((tiles, TILE, ch), BF16),
            V((hid_n, 2 * ch), BF16),
            V((tiles, hid_n, TILE), F32),
            V((tiles, hid_n, TILE), F32),
            V((tiles, hid_n, TILE), BF16),
            V((line, hid_n, 2 * rows), F32),
            V((line, 2 * rows, ch), F32),
            V((nb, ch, blk), F32),
            V((nb * slots + 1, ch, blk), F32),
            V((nb, blk, ch), BF16),
            V((line, 2, rows, wide), F32),
            V((line, 2, rows, wide), BF16),
            V((line, rows, wide), BF16),
            V((line, n_grp, share, wide), F32),
            V((line, n_grp, share, wide), BF16),
            V((n_grp - 1, line, share, wide), BF16),
            V((line - 1, share, wide), BF16),
            V((line - 1, share, wide), BF16),
            V((n_grp, share, wide), BF16),
            dma((6,)), dma((3,)),
            dma((n_dom, exports, 3)), dma((n_dom, exports)),
            dma((line,)), dma((line,)),
            dma((n_grp - 1, line)), dma((n_grp - 1, line)),
            dma((line - 1,)), dma((line - 1,)),
            dma((n_grp - 1,)), dma((n_grp - 1,)),
        ],
        compiler_params=pltpu.CompilerParams(
            collective_id=0, has_side_effects=True, vmem_limit_bytes=56 * 2**20
        ),
        cost_estimate=cost,
    )(
        targets, counts, prev, last_of, wanted, features.reshape(nb, blk, ch), boundary_cache, adjacency,
        weight_in, weight_out, cotangent.reshape(tiles, TILE, ch),
    )
    scale = 1.0 / math.sqrt(node_rows * n_grp * n_dom)
    gw_in, gw_out = (x.reshape(rows, -1).astype(F32) * scale for x in (gw_in, gw_out))
    return out.reshape(node_rows, ch), gw_in, gw_out


def local(
    features, boundary_cache, adjacency, neighbor, counts, wanted, weight_in, weight_out, cotangent
):
    nblocks = adjacency.shape[0]
    slot_total = adjacency.shape[1]
    block_rows = adjacency.shape[2]
    channels = features.shape[1]
    node_rows = nblocks * block_rows
    partners = lax.axis_size("dom")
    cache_copy = boundary_cache.astype(jnp.bfloat16)
    exported = cache_copy.reshape(-1, block_rows, channels)
    export_total = exported.shape[0]
    exported_all = lax.all_gather(cache_copy, "dom", axis=0, tiled=True).reshape(
        partners, export_total, block_rows, channels
    )
    selected = wanted[0]
    boundary = exported_all[:, 0]
    boundary = jnp.where((selected == 1)[:, None, None], exported_all[:, 1], boundary)
    owned = features.reshape(nblocks, block_rows, channels)
    sources = jnp.concatenate([owned, boundary], 0)
    active = jnp.arange(slot_total)[None, :] < counts[:, None]
    chosen = sources[neighbor]
    chosen = jnp.where(active[:, :, None, None], chosen, jnp.zeros_like(chosen))
    aggregate = jnp.einsum("bsij,bsjf->bif", adjacency, chosen, preferred_element_type=jnp.float32)
    aggregate = aggregate.astype(jnp.bfloat16).reshape(node_rows, channels)
    joined = jnp.concatenate([aggregate, features], 1)
    preact = jnp.dot(joined, weight_in, preferred_element_type=jnp.float32)
    gating = jax.nn.sigmoid(preact)
    hidden = (preact * gating).astype(jnp.bfloat16)
    grad_hidden = jnp.einsum("nf,hf->nh", cotangent, weight_out, preferred_element_type=jnp.float32)
    grad_preact = (grad_hidden * gating * (1.0 + preact * (1.0 - gating))).astype(jnp.bfloat16)
    grad_joined = jnp.einsum(
        "nh,ch->nc", grad_preact, weight_in, preferred_element_type=jnp.float32
    )
    grad_aggregate = (
        grad_joined[:, :channels].astype(jnp.bfloat16).reshape(nblocks, block_rows, channels)
    )
    backward = jnp.einsum(
        "bsji,bjf->bsif", adjacency, grad_aggregate, preferred_element_type=jnp.float32
    )
    local_hit = active & (neighbor < nblocks)
    routing = (neighbor[None, :, :] == jnp.arange(nblocks)[:, None, None]) & local_hit[None]
    spread = jnp.einsum(
        "cbs,bsif->cif", routing.astype(jnp.float32), backward, precision=lax.Precision.HIGHEST
    )
    grad_features = (grad_joined[:, channels:] + spread.reshape(node_rows, channels)).astype(
        jnp.bfloat16
    )
    node_total = node_rows * lax.axis_size("grp") * partners
    loss_scale = 1.0 / math.sqrt(node_total)
    rows_in = weight_in.shape[0] // partners
    rows_out = weight_out.shape[0] // partners
    summed = lax.psum(
        (
            jnp.einsum("nc,nh->ch", joined, grad_preact, preferred_element_type=jnp.float32)
            * loss_scale,
            jnp.einsum("nh,nf->hf", hidden, cotangent, preferred_element_type=jnp.float32)
            * loss_scale,
        ),
        ("grp", "dom"),
    )
    position = lax.axis_index("dom")
    grad_weight_in = lax.dynamic_slice_in_dim(summed[0], position * rows_in, rows_in, 0)
    grad_weight_out = lax.dynamic_slice_in_dim(summed[1], position * rows_out, rows_out, 0)
    return (grad_features, grad_weight_in, grad_weight_out)


def solution(mesh):
    in_specs = (
        P(("grp", "dom"), None),
        P(("grp", "dom"), None),
        P(("grp", "dom"), None, None, None),
        P(("grp", "dom"), None),
        P(("grp", "dom")),
        P(("grp", "dom"), None),
        P(),
        P(),
        P(("grp", "dom"), None),
    )
    out_specs = (P(("grp", "dom"), None), P("dom", None), P("dom", None))
    n_grp, n_dom = mesh.shape["grp"], mesh.shape["dom"]

    def program(*args):
        rows = args[7].shape[0] // n_dom
        nodes = args[0].shape[0] // (n_grp * n_dom)
        fits = rows % (16 * n_grp) == 0 and (2 * rows) % 128 == 0 and nodes % TILE == 0
        body = fast_local if fits else local
        return sharded(body)(*args)

    def sharded(body):
        return jax.shard_map(
            body, mesh=mesh, in_specs=in_specs, out_specs=out_specs, check_vma=False
        )

    return program
```

```python
import functools
import math

import jax
import jax.numpy as jnp
from jax import lax
from jax.experimental import pallas as pl
from jax.experimental.pallas import tpu as pltpu
from jax.sharding import PartitionSpec as P

F32, BF16 = jnp.float32, jnp.bfloat16
TILE = 512
NT_DIMS = (((1,), (1,)), ((), ()))


def mm(a, b):
    return jnp.dot(a, b, preferred_element_type=F32)


def mm_nt(a, b):
    return lax.dot_general(a, b, NT_DIMS, preferred_element_type=F32)


def layer_kernel(
    n_grp, n_dom,
    nbr, cnt, wnt, feat_h, cache_h, adj_h, win_h, wout_h, cot_h,
    out_h, gw_h,
    src, cache, adj, win, wout, cot, win_t, pre2, gh, gps, hids, aggs, acc_in, acc_out,
    base, terms, out, own1, sb1, rb1, chip, sb2, rb2, sb3, rb3, gat4, table, links,
    load_sem, out_sem, b_send, b_recv, s1, r1, s2, r2, s3, r3, s4, r4,
):
    nb, slots, blk, _ = adj.shape
    exports = cache.shape[0] // blk
    line = n_dom // 2
    tiles = cot.shape[0]
    per = TILE // blk
    ch = cot.shape[2]
    hid_n = wout.shape[0]
    rows = rb1.shape[1]
    none = nb + n_dom * exports

    g = lax.axis_index("grp")
    d = lax.axis_index("dom")
    z, c = d // 2, lax.rem(d, 2)
    pair = z * 2 + (1 - c)

    def load(i, a, b):
        return pltpu.make_async_copy(a, b, load_sem.at[i])

    loads = [
        load(0, cache_h, cache),
        load(1, wout_h, wout),
        load(2, cot_h, cot),
        load(3, win_h, win),
        load(4, feat_h, src.at[pl.ds(0, nb)]),
        load(5, adj_h, adj),
    ]
    for item in loads:
        item.start()

    barrier = pltpu.get_barrier_semaphore()
    peers = [(g, pair)]
    peers += [(g, 2 * lax.rem(z + k, line) + c) for k in range(1, line)]
    peers += [(lax.rem(g + k, n_grp), d) for k in range(1, n_grp)]
    for peer in peers:
        pl.semaphore_signal(barrier, inc=1, device_id=peer, device_id_type=pl.DeviceIdType.MESH)

    loads[0].wait()
    src[pl.ds(nb + d * exports, exports)] = cache[...].astype(BF16).reshape(exports, blk, ch)
    pl.semaphore_wait(barrier, len(peers))

    def remote(a, b, send, recv, where):
        return pltpu.make_async_remote_copy(
            src_ref=a, dst_ref=b, send_sem=send, recv_sem=recv,
            device_id=where, device_id_type=pl.DeviceIdType.MESH,
        )

    def spread(q, e, way):
        part = src.at[nb + q * exports + e]
        to = (d + 2, d - 2, pair)[way]
        return remote(part, part, b_send.at[q, e, way], b_recv.at[q, e], (g, to))

    not_last, not_first = z < line - 1, z > 0
    for e in range(exports):
        pl.when(not_last)(lambda: spread(d, e, 0).start())
        pl.when(not_first)(lambda: spread(d, e, 1).start())
    for e in range(exports):
        spread(d, e, 2).start()

    pairs = nb * slots
    lane = lax.broadcasted_iota(jnp.int32, table.shape, 1)

    def target(b, s):
        return jnp.where(s < cnt[b], nbr[s, b], nb + n_dom)

    def ask(b, asked):
        for s in range(slots):
            asked = jnp.where(lane == b * slots + s, target(b, s), asked)
        return asked

    def find(b, found):
        for s in range(slots):
            p = b * slots + s
            hit = jnp.logical_and(asked == target(b, s), limit > p)
            found = jnp.where(hit, p + 1, found)
        return found

    limit = jnp.minimum(lane, pairs)
    asked = lax.fori_loop(0, nb, ask, lane - pairs)
    table[...] = lax.fori_loop(0, nb, find, jnp.zeros_like(lane))
    to_links = load(6, table, links)
    to_links.start()

    for item in loads[1:5]:
        item.wait()
    win_t[...] = win[...].astype(F32).T.astype(BF16)
    src[pl.ds(none, exports)] = jnp.zeros((exports, blk, ch), BF16)
    terms[0] = jnp.zeros((ch, blk), F32)

    def early(i, carry):
        gh[i] = mm_nt(wout[...], cot[i])
        own = src[pl.ds(i * per, per)].reshape(TILE, ch)
        pre2[i] = mm_nt(win_t[:, ch:], own)
        return carry

    done = 0
    for k in range(1, line):
        upto = tiles * k // (line - 1)
        lax.fori_loop(done, upto, early, 0)
        done = upto

        @pl.when(z - k >= 0)
        def _():
            for e in range(exports):
                spread(d - 2 * k, e, 0).wait_recv()
                pl.when(not_last)(lambda: spread(d - 2 * k, e, 0).start())
                spread(d - 2 * k, e, 2).start()

        @pl.when(z + k < line)
        def _():
            for e in range(exports):
                spread(d + 2 * k, e, 1).wait_recv()
                pl.when(not_first)(lambda: spread(d + 2 * k, e, 1).start())
                spread(d + 2 * k, e, 2).start()

    acc_in[...] = jnp.zeros_like(acc_in)
    acc_out[...] = jnp.zeros_like(acc_out)
    loads[5].wait()
    to_links.wait()
    for zz in range(line):
        for e in range(exports):
            spread(2 * zz + 1 - c, e, 2).wait_recv()

    def source(b, s):
        n = target(b, s)
        far = jnp.maximum(n - nb, 0)
        pick = wnt[0, jnp.minimum(far, n_dom - 1)]
        return src[jnp.where(n < nb, n, nb + far * exports + pick)]

    def front(i):
        parts = []
        for k in range(per):
            b = i * per + k
            left = jnp.concatenate([adj[b, s] for s in range(slots)], axis=1)
            right = jnp.concatenate([source(b, s) for s in range(slots)], axis=0)
            parts.append(mm(left, right).astype(BF16))
        agg = jnp.concatenate(parts, axis=0)
        pre = pre2[i] + mm_nt(win_t[:, :ch], agg)
        sg = 0.5 + 0.5 * jnp.tanh(0.5 * pre)
        h = pre * sg
        gps[i] = (gh[i] * (sg + h * (1.0 - sg))).astype(BF16)
        hids[i] = h.astype(BF16)
        aggs[i] = agg

    def weight_grads(i):
        gp = gps[i]
        own = src[pl.ds(i * per, per)].reshape(TILE, ch)
        for m, part in enumerate((aggs[i], own)):
            term = mm(gp, part)
            for j in range(ch // (2 * rows)):
                at = m * (ch // (2 * rows)) + j
                acc_in[at] += term[:, j * 2 * rows : (j + 1) * 2 * rows]
        acc_out[...] += mm(hids[i], cot[i]).reshape(acc_out.shape)

    def main(i, carry):
        weight_grads(i - 1)
        front(i)
        return carry

    front(0)
    lax.fori_loop(1, tiles, main, 0)
    weight_grads(tiles - 1)

    def late(i, carry):
        gj = mm(win[...], gps[i])
        gagg = gj[:ch].astype(BF16)
        for k in range(per):
            b = i * per + k
            cols = slice(k * blk, (k + 1) * blk)
            base[b] = gj[ch:, cols]
            both = mm(gagg[:, cols], jnp.concatenate([adj[b, s] for s in range(slots)], axis=1))
            for s in range(slots):
                terms[1 + b * slots + s] = both[:, s * blk : (s + 1) * blk]
        return carry

    def chain(b, carry):
        for s in range(slots):
            terms[1 + b * slots + s] += terms[links[0, b * slots + s]]
        return carry

    def write(b, carry):
        out[b] = (base[b] + terms[links[0, pairs + b]]).T.astype(BF16)
        return carry

    order = [lax.rem(z + k, line) for k in range(1, line + 1)]

    def step1(zz):
        return remote(sb1.at[zz, 1 - c], rb1.at[zz], s1.at[zz], r1.at[zz], (g, pair))

    for zz in order:
        whole = jnp.concatenate([acc_in[zz].T, acc_out[zz]], axis=1)
        whole = whole.reshape(2, rows, whole.shape[1])
        own1[zz] = whole
        sb1[zz] = whole.astype(BF16)
        step1(zz).start()

    def step2(zz, k):
        to = lax.rem(g + k, n_grp)
        return remote(
            sb2.at[zz, to], rb2.at[k - 1, zz], s2.at[k - 1, zz], r2.at[k - 1, zz], (to, d)
        )

    for zz in order:
        step1(zz).wait_recv()
        both = (own1[zz, c] + rb1[zz].astype(F32)).reshape(chip.shape[1:])
        chip[zz] = both
        sb2[zz] = both.astype(BF16)
        for k in range(1, n_grp):
            step2(zz, k).start()

    lax.fori_loop(0, tiles, late, 0)
    def step3(k):
        to = lax.rem(z + k, line)
        return remote(sb3.at[k - 1], rb3.at[k - 1], s3.at[k - 1], r3.at[k - 1], (g, 2 * to + c))

    total = None
    for k, zz in enumerate(order, 1):
        total = chip[zz, g]
        for j in range(1, n_grp):
            step2(zz, j).wait_recv()
            total += rb2[j - 1, zz].astype(F32)
        if k < line:
            sb3[k - 1] = total.astype(BF16)
            step3(k).start()
    lax.fori_loop(0, nb, chain, 0)
    for k in range(1, line):
        step3(k).wait_recv()
        total += rb3[k - 1].astype(F32)

    def step4(k):
        to = lax.rem(g + k, n_grp)
        return remote(gat4.at[g], gat4.at[g], s4.at[k - 1], r4.at[k - 1], (to, d))

    def arrive4(k):
        there = gat4.at[lax.rem(g - k + n_grp, n_grp)]
        return remote(there, there, s4.at[k - 1], r4.at[k - 1], (lax.rem(g + k, n_grp), d))

    gat4[g] = total.astype(BF16)
    for k in range(1, n_grp):
        step4(k).start()
    lax.fori_loop(0, nb, write, 0)
    store = pltpu.make_async_copy(out, out_h, out_sem.at[0])
    store.start()
    for k in range(1, n_grp):
        arrive4(k).wait_recv()
    last = pltpu.make_async_copy(gat4, gw_h, out_sem.at[1])
    last.start()

    for e in range(exports):
        pl.when(not_last)(lambda: spread(d, e, 0).wait_send())
        pl.when(not_first)(lambda: spread(d, e, 1).wait_send())
        spread(d, e, 2).wait_send()
    for k in range(1, line):

        @pl.when(z - k >= 0)
        def _():
            for e in range(exports):
                pl.when(not_last)(lambda: spread(d - 2 * k, e, 0).wait_send())
                spread(d - 2 * k, e, 2).wait_send()

        @pl.when(z + k < line)
        def _():
            for e in range(exports):
                pl.when(not_first)(lambda: spread(d + 2 * k, e, 1).wait_send())
                spread(d + 2 * k, e, 2).wait_send()

    for zz in order:
        step1(zz).wait_send()
        for k in range(1, n_grp):
            step2(zz, k).wait_send()
    for k in range(1, line):
        step3(k).wait_send()
    for k in range(1, n_grp):
        step4(k).wait_send()
    store.wait()
    last.wait()


def finish_kernel(scale, out_a, in_a, out_b, gw_in, gw_out, sems):
    count = sems.shape[0]
    step = out_a.shape[0] // count
    copies = []
    for i in range(count):
        part = pl.ds(i * step, step)
        copies.append(pltpu.make_async_copy(out_a.at[part], out_b.at[part], sems.at[i]))
    for item in copies:
        item.start()
    value = in_a[...].astype(F32) * scale
    gw_in[...] = value[:, : gw_in.shape[1]]
    gw_out[...] = value[:, gw_in.shape[1] :]
    for item in copies:
        item.wait()


def fast_local(
    features, boundary_cache, adjacency, neighbor, counts, wanted, weight_in, weight_out, cotangent
):
    nb, slots, blk, _ = adjacency.shape
    node_rows, ch = features.shape
    hid_n = weight_out.shape[0]
    n_grp, n_dom = lax.axis_size("grp"), lax.axis_size("dom")
    line = n_dom // 2
    tiles = node_rows // TILE
    exports = boundary_cache.shape[0] // blk
    rows = hid_n // n_dom
    wide = hid_n + ch
    share = rows // n_grp
    links_wide = -(-(nb * slots + nb) // 128) * 128
    any_spec = pl.BlockSpec(memory_space=pl.ANY)
    vmem = pl.BlockSpec(memory_space=pltpu.VMEM)
    smem = pl.BlockSpec(memory_space=pltpu.SMEM)
    dma = pltpu.SemaphoreType.DMA
    V = pltpu.VMEM
    nodes = node_rows
    cost = pl.CostEstimate(
        flops=2 * nodes * hid_n * (7 * ch), bytes_accessed=8 * nodes * ch,
        transcendentals=nodes * hid_n,
    )
    out, gw = pl.pallas_call(
        functools.partial(layer_kernel, n_grp, n_dom),
        out_shape=(
            jax.ShapeDtypeStruct((nb, blk, ch), BF16),
            jax.ShapeDtypeStruct((n_grp, share, wide), BF16),
        ),
        in_specs=[smem] * 3 + [any_spec] * 6,
        out_specs=(any_spec,) * 2,
        scratch_shapes=[
            V((nb + (n_dom + 1) * exports, blk, ch), BF16),
            V(boundary_cache.shape, F32),
            V(adjacency.shape, BF16),
            V(weight_in.shape, BF16),
            V(weight_out.shape, BF16),
            V((tiles, TILE, ch), BF16),
            V((hid_n, 2 * ch), BF16),
            V((tiles, hid_n, TILE), F32),
            V((tiles, hid_n, TILE), F32),
            V((tiles, hid_n, TILE), BF16),
            V((tiles, hid_n, TILE), BF16),
            V((tiles, TILE, ch), BF16),
            V((line, hid_n, 2 * rows), F32),
            V((line, 2 * rows, ch), F32),
            V((nb, ch, blk), F32),
            V((nb * slots + 1, ch, blk), F32),
            V((nb, blk, ch), BF16),
            V((line, 2, rows, wide), F32),
            V((line, 2, rows, wide), BF16),
            V((line, rows, wide), BF16),
            V((line, n_grp, share, wide), F32),
            V((line, n_grp, share, wide), BF16),
            V((n_grp - 1, line, share, wide), BF16),
            V((line - 1, share, wide), BF16),
            V((line - 1, share, wide), BF16),
            V((n_grp, share, wide), BF16),
            V((8, links_wide), jnp.int32), pltpu.SMEM((8, links_wide), jnp.int32),
            dma((7,)), dma((2,)),
            dma((n_dom, exports, 3)), dma((n_dom, exports)),
            dma((line,)), dma((line,)),
            dma((n_grp - 1, line)), dma((n_grp - 1, line)),
            dma((line - 1,)), dma((line - 1,)),
            dma((n_grp - 1,)), dma((n_grp - 1,)),
        ],
        compiler_params=pltpu.CompilerParams(
            collective_id=0, has_side_effects=True, vmem_limit_bytes=56 * 2**20
        ),
        cost_estimate=cost,
    )(
        neighbor.T, counts, wanted, features.reshape(nb, blk, ch), boundary_cache, adjacency,
        weight_in, weight_out, cotangent.reshape(tiles, TILE, ch),
    )
    scale = 1.0 / math.sqrt(node_rows * n_grp * n_dom)
    out, gw_in, gw_out = pl.pallas_call(
        functools.partial(finish_kernel, scale),
        out_shape=(
            jax.ShapeDtypeStruct((node_rows, ch), BF16),
            jax.ShapeDtypeStruct((rows, hid_n), F32),
            jax.ShapeDtypeStruct((rows, ch), F32),
        ),
        in_specs=[any_spec, vmem],
        out_specs=(any_spec, vmem, vmem),
        scratch_shapes=[dma((8 if node_rows % 128 == 0 else 1,))],
        compiler_params=pltpu.CompilerParams(vmem_limit_bytes=56 * 2**20),
    )(out.reshape(node_rows, ch), gw.reshape(rows, wide))
    return out, gw_in, gw_out


def local(
    features, boundary_cache, adjacency, neighbor, counts, wanted, weight_in, weight_out, cotangent
):
    nblocks = adjacency.shape[0]
    slot_total = adjacency.shape[1]
    block_rows = adjacency.shape[2]
    channels = features.shape[1]
    node_rows = nblocks * block_rows
    partners = lax.axis_size("dom")
    cache_copy = boundary_cache.astype(jnp.bfloat16)
    exported = cache_copy.reshape(-1, block_rows, channels)
    export_total = exported.shape[0]
    exported_all = lax.all_gather(cache_copy, "dom", axis=0, tiled=True).reshape(
        partners, export_total, block_rows, channels
    )
    selected = wanted[0]
    boundary = exported_all[:, 0]
    boundary = jnp.where((selected == 1)[:, None, None], exported_all[:, 1], boundary)
    owned = features.reshape(nblocks, block_rows, channels)
    sources = jnp.concatenate([owned, boundary], 0)
    active = jnp.arange(slot_total)[None, :] < counts[:, None]
    chosen = sources[neighbor]
    chosen = jnp.where(active[:, :, None, None], chosen, jnp.zeros_like(chosen))
    aggregate = jnp.einsum("bsij,bsjf->bif", adjacency, chosen, preferred_element_type=jnp.float32)
    aggregate = aggregate.astype(jnp.bfloat16).reshape(node_rows, channels)
    joined = jnp.concatenate([aggregate, features], 1)
    preact = jnp.dot(joined, weight_in, preferred_element_type=jnp.float32)
    gating = jax.nn.sigmoid(preact)
    hidden = (preact * gating).astype(jnp.bfloat16)
    grad_hidden = jnp.einsum("nf,hf->nh", cotangent, weight_out, preferred_element_type=jnp.float32)
    grad_preact = (grad_hidden * gating * (1.0 + preact * (1.0 - gating))).astype(jnp.bfloat16)
    grad_joined = jnp.einsum(
        "nh,ch->nc", grad_preact, weight_in, preferred_element_type=jnp.float32
    )
    grad_aggregate = (
        grad_joined[:, :channels].astype(jnp.bfloat16).reshape(nblocks, block_rows, channels)
    )
    backward = jnp.einsum(
        "bsji,bjf->bsif", adjacency, grad_aggregate, preferred_element_type=jnp.float32
    )
    local_hit = active & (neighbor < nblocks)
    routing = (neighbor[None, :, :] == jnp.arange(nblocks)[:, None, None]) & local_hit[None]
    spread = jnp.einsum(
        "cbs,bsif->cif", routing.astype(jnp.float32), backward, precision=lax.Precision.HIGHEST
    )
    grad_features = (grad_joined[:, channels:] + spread.reshape(node_rows, channels)).astype(
        jnp.bfloat16
    )
    node_total = node_rows * lax.axis_size("grp") * partners
    loss_scale = 1.0 / math.sqrt(node_total)
    rows_in = weight_in.shape[0] // partners
    rows_out = weight_out.shape[0] // partners
    summed = lax.psum(
        (
            jnp.einsum("nc,nh->ch", joined, grad_preact, preferred_element_type=jnp.float32)
            * loss_scale,
            jnp.einsum("nh,nf->hf", hidden, cotangent, preferred_element_type=jnp.float32)
            * loss_scale,
        ),
        ("grp", "dom"),
    )
    position = lax.axis_index("dom")
    grad_weight_in = lax.dynamic_slice_in_dim(summed[0], position * rows_in, rows_in, 0)
    grad_weight_out = lax.dynamic_slice_in_dim(summed[1], position * rows_out, rows_out, 0)
    return (grad_features, grad_weight_in, grad_weight_out)


def solution(mesh):
    in_specs = (
        P(("grp", "dom"), None),
        P(("grp", "dom"), None),
        P(("grp", "dom"), None, None, None),
        P(("grp", "dom"), None),
        P(("grp", "dom")),
        P(("grp", "dom"), None),
        P(),
        P(),
        P(("grp", "dom"), None),
    )
    out_specs = (P(("grp", "dom"), None), P("dom", None), P("dom", None))
    n_grp, n_dom = mesh.shape["grp"], mesh.shape["dom"]

    def program(*args):
        rows = args[7].shape[0] // n_dom
        nodes = args[0].shape[0] // (n_grp * n_dom)
        fits = rows % (16 * n_grp) == 0 and (2 * rows) % 128 == 0 and nodes % TILE == 0
        body = fast_local if fits else local
        return sharded(body)(*args)

    def sharded(body):
        return jax.shard_map(
            body, mesh=mesh, in_specs=in_specs, out_specs=out_specs, check_vma=False
        )

    return program
```

```python
import functools
import math

import jax
import jax.numpy as jnp
from jax import lax
from jax.experimental import pallas as pl
from jax.experimental.pallas import tpu as pltpu
from jax.sharding import PartitionSpec as P

F32, BF16 = jnp.float32, jnp.bfloat16
TILE = 512
NT_DIMS = (((1,), (1,)), ((), ()))


def mm(a, b):
    return jnp.dot(a, b, preferred_element_type=F32)


def mm_nt(a, b):
    return lax.dot_general(a, b, NT_DIMS, preferred_element_type=F32)


def layer_kernel(
    n_grp, n_dom,
    nbr, cnt, wnt, feat_h, cache_h, adj_h, win_h, wout_h, cot_h,
    out_h, gw_h,
    src, cache, adj, win, wout, cot, win_t, pre2, gh, gps, hids, aggs, acc_in, acc_out,
    base, terms, out, own1, sb1, rb1, chip, sb2, rb2, sb3, rb3, gat4, table, links,
    load_sem, out_sem, b_send, b_recv, s1, r1, s2, r2, s3, r3, s4, r4,
):
    nb, slots, blk, _ = adj.shape
    exports = cache.shape[0] // blk
    line = n_dom // 2
    tiles = cot.shape[0]
    per = TILE // blk
    ch = cot.shape[2]
    hid_n = wout.shape[0]
    rows = rb1.shape[1]
    none = nb + n_dom * exports

    g = lax.axis_index("grp")
    d = lax.axis_index("dom")
    z, c = d // 2, lax.rem(d, 2)
    pair = z * 2 + (1 - c)

    def load(i, a, b):
        return pltpu.make_async_copy(a, b, load_sem.at[i])

    loads = [
        load(0, cache_h, cache),
        load(1, wout_h, wout),
        load(2, cot_h, cot),
        load(3, win_h, win),
        load(4, feat_h, src.at[pl.ds(0, nb)]),
        load(5, adj_h, adj),
    ]
    for item in loads:
        item.start()

    barrier = pltpu.get_barrier_semaphore()
    peers = [(g, pair)]
    peers += [(g, 2 * lax.rem(z + k, line) + c) for k in range(1, line)]
    peers += [(lax.rem(g + k, n_grp), d) for k in range(1, n_grp)]
    for peer in peers:
        pl.semaphore_signal(barrier, inc=1, device_id=peer, device_id_type=pl.DeviceIdType.MESH)

    loads[0].wait()
    src[pl.ds(nb + d * exports, exports)] = cache[...].astype(BF16).reshape(exports, blk, ch)
    pl.semaphore_wait(barrier, len(peers))

    def remote(a, b, send, recv, where):
        return pltpu.make_async_remote_copy(
            src_ref=a, dst_ref=b, send_sem=send, recv_sem=recv,
            device_id=where, device_id_type=pl.DeviceIdType.MESH,
        )

    def spread(q, e, way):
        part = src.at[nb + q * exports + e]
        to = (d + 2, d - 2, pair)[way]
        return remote(part, part, b_send.at[q, e, way], b_recv.at[q, e], (g, to))

    not_last, not_first = z < line - 1, z > 0
    for e in range(exports):
        pl.when(not_last)(lambda: spread(d, e, 0).start())
        pl.when(not_first)(lambda: spread(d, e, 1).start())
    for e in range(exports):
        spread(d, e, 2).start()

    pairs = nb * slots
    lane = lax.broadcasted_iota(jnp.int32, table.shape, 1)

    def target(b, s):
        return jnp.where(s < cnt[b], nbr[s, b], nb + n_dom)

    def ask(b, asked):
        for s in range(slots):
            asked = jnp.where(lane == b * slots + s, target(b, s), asked)
        return asked

    def find(b, found):
        for s in range(slots):
            p = b * slots + s
            hit = jnp.logical_and(asked == target(b, s), limit > p)
            found = jnp.where(hit, p + 1, found)
        return found

    for item in loads[1:5]:
        item.wait()
    win_t[...] = win[...].astype(F32).T.astype(BF16)
    src[pl.ds(none, exports)] = jnp.zeros((exports, blk, ch), BF16)
    terms[0] = jnp.zeros((ch, blk), F32)

    def early(i, carry):
        gh[i] = mm_nt(wout[...], cot[i])
        own = src[pl.ds(i * per, per)].reshape(TILE, ch)
        pre2[i] = mm_nt(win_t[:, ch:], own)
        return carry

    done = 0
    for k in range(1, line):
        upto = max(0, (tiles * k - 1) // line)
        lax.fori_loop(done, upto, early, 0)
        done = upto

        @pl.when(z - k >= 0)
        def _():
            for e in range(exports):
                spread(d - 2 * k, e, 0).wait_recv()
                pl.when(not_last)(lambda: spread(d - 2 * k, e, 0).start())
                spread(d - 2 * k, e, 2).start()

        @pl.when(z + k < line)
        def _():
            for e in range(exports):
                spread(d + 2 * k, e, 1).wait_recv()
                pl.when(not_first)(lambda: spread(d + 2 * k, e, 1).start())
                spread(d + 2 * k, e, 2).start()

    limit = jnp.minimum(lane, pairs)
    asked = lax.fori_loop(0, nb, ask, lane - pairs)
    table[...] = lax.fori_loop(0, nb, find, jnp.zeros_like(lane))
    to_links = load(6, table, links)
    to_links.start()

    lax.fori_loop(done, tiles, early, 0)
    acc_in[...] = jnp.zeros_like(acc_in)
    acc_out[...] = jnp.zeros_like(acc_out)
    loads[5].wait()
    to_links.wait()
    for zz in range(line):
        for e in range(exports):
            spread(2 * zz + 1 - c, e, 2).wait_recv()

    def source(b, s):
        n = target(b, s)
        far = jnp.maximum(n - nb, 0)
        pick = wnt[0, jnp.minimum(far, n_dom - 1)]
        return src[jnp.where(n < nb, n, nb + far * exports + pick)]

    def front(i):
        parts = []
        for k in range(per):
            b = i * per + k
            left = jnp.concatenate([adj[b, s] for s in range(slots)], axis=1)
            right = jnp.concatenate([source(b, s) for s in range(slots)], axis=0)
            parts.append(mm(left, right).astype(BF16))
        agg = jnp.concatenate(parts, axis=0)
        pre = pre2[i] + mm_nt(win_t[:, :ch], agg)
        sg = 0.5 + 0.5 * jnp.tanh(0.5 * pre)
        h = pre * sg
        gps[i] = (gh[i] * (sg + h * (1.0 - sg))).astype(BF16)
        hids[i] = h.astype(BF16)
        aggs[i] = agg

    def weight_grads(i):
        gp = gps[i]
        own = src[pl.ds(i * per, per)].reshape(TILE, ch)
        for m, part in enumerate((aggs[i], own)):
            term = mm(gp, part)
            for j in range(ch // (2 * rows)):
                at = m * (ch // (2 * rows)) + j
                acc_in[at] += term[:, j * 2 * rows : (j + 1) * 2 * rows]
        acc_out[...] += mm(hids[i], cot[i]).reshape(acc_out.shape)

    def main(i, carry):
        weight_grads(i - 1)
        front(i)
        return carry

    front(0)
    lax.fori_loop(1, tiles, main, 0)
    weight_grads(tiles - 1)

    def late(i, carry):
        gj = mm(win[...], gps[i])
        gagg = gj[:ch].astype(BF16)
        for k in range(per):
            b = i * per + k
            cols = slice(k * blk, (k + 1) * blk)
            base[b] = gj[ch:, cols]
            both = mm(gagg[:, cols], jnp.concatenate([adj[b, s] for s in range(slots)], axis=1))
            for s in range(slots):
                terms[1 + b * slots + s] = both[:, s * blk : (s + 1) * blk]
        return carry

    def chain(b, carry):
        for s in range(slots):
            terms[1 + b * slots + s] += terms[links[0, b * slots + s]]
        return carry

    def write(b, carry):
        out[b] = (base[b] + terms[links[0, pairs + b]]).T.astype(BF16)
        return carry

    order = [lax.rem(z + k, line) for k in range(1, line + 1)]

    def step1(zz):
        return remote(sb1.at[zz, 1 - c], rb1.at[zz], s1.at[zz], r1.at[zz], (g, pair))

    for zz in order:
        whole = jnp.concatenate([acc_in[zz].T, acc_out[zz]], axis=1)
        whole = whole.reshape(2, rows, whole.shape[1])
        own1[zz] = whole
        sb1[zz] = whole.astype(BF16)
        step1(zz).start()

    def step2(zz, k):
        to = lax.rem(g + k, n_grp)
        return remote(
            sb2.at[zz, to], rb2.at[k - 1, zz], s2.at[k - 1, zz], r2.at[k - 1, zz], (to, d)
        )

    for zz in order:
        step1(zz).wait_recv()
        both = (own1[zz, c] + rb1[zz].astype(F32)).reshape(chip.shape[1:])
        chip[zz] = both
        sb2[zz] = both.astype(BF16)
        for k in range(1, n_grp):
            step2(zz, k).start()

    lax.fori_loop(0, tiles, late, 0)
    lax.fori_loop(0, nb, chain, 0)
    def step3(k):
        to = lax.rem(z + k, line)
        return remote(sb3.at[k - 1], rb3.at[k - 1], s3.at[k - 1], r3.at[k - 1], (g, 2 * to + c))

    total = None
    for k, zz in enumerate(order, 1):
        total = chip[zz, g]
        for j in range(1, n_grp):
            step2(zz, j).wait_recv()
            total += rb2[j - 1, zz].astype(F32)
        if k < line:
            sb3[k - 1] = total.astype(BF16)
            step3(k).start()
    lax.fori_loop(0, nb, write, 0)
    store = pltpu.make_async_copy(out, out_h, out_sem.at[0])
    store.start()
    for k in range(1, line):
        step3(k).wait_recv()
        total += rb3[k - 1].astype(F32)

    def step4(k):
        to = lax.rem(g + k, n_grp)
        return remote(gat4.at[g], gat4.at[g], s4.at[k - 1], r4.at[k - 1], (to, d))

    def arrive4(k):
        there = gat4.at[lax.rem(g - k + n_grp, n_grp)]
        return remote(there, there, s4.at[k - 1], r4.at[k - 1], (lax.rem(g + k, n_grp), d))

    gat4[g] = total.astype(BF16)
    for k in range(1, n_grp):
        step4(k).start()
    for k in range(1, n_grp):
        arrive4(k).wait_recv()
    last = pltpu.make_async_copy(gat4, gw_h, out_sem.at[1])
    last.start()

    for e in range(exports):
        pl.when(not_last)(lambda: spread(d, e, 0).wait_send())
        pl.when(not_first)(lambda: spread(d, e, 1).wait_send())
        spread(d, e, 2).wait_send()
    for k in range(1, line):

        @pl.when(z - k >= 0)
        def _():
            for e in range(exports):
                pl.when(not_last)(lambda: spread(d - 2 * k, e, 0).wait_send())
                spread(d - 2 * k, e, 2).wait_send()

        @pl.when(z + k < line)
        def _():
            for e in range(exports):
                pl.when(not_first)(lambda: spread(d + 2 * k, e, 1).wait_send())
                spread(d + 2 * k, e, 2).wait_send()

    for zz in order:
        step1(zz).wait_send()
        for k in range(1, n_grp):
            step2(zz, k).wait_send()
    for k in range(1, line):
        step3(k).wait_send()
    for k in range(1, n_grp):
        step4(k).wait_send()
    store.wait()
    last.wait()


def finish_kernel(scale, out_a, in_a, out_b, gw_in, gw_out, held, in_sems, out_sems):
    count = in_sems.shape[0]
    step = out_a.shape[0] // count
    parts = [pl.ds(i * step, step) for i in range(count)]
    loads = [
        pltpu.make_async_copy(out_a.at[p], held.at[p], in_sems.at[i]) for i, p in enumerate(parts)
    ]
    stores = [
        pltpu.make_async_copy(held.at[p], out_b.at[p], out_sems.at[i]) for i, p in enumerate(parts)
    ]
    for item in loads:
        item.start()
    value = in_a[...].astype(F32) * scale
    gw_in[...] = value[:, : gw_in.shape[1]]
    gw_out[...] = value[:, gw_in.shape[1] :]
    for load, store in zip(loads, stores):
        load.wait()
        store.start()
    for item in stores:
        item.wait()


def fast_local(
    features, boundary_cache, adjacency, neighbor, counts, wanted, weight_in, weight_out, cotangent
):
    nb, slots, blk, _ = adjacency.shape
    node_rows, ch = features.shape
    hid_n = weight_out.shape[0]
    n_grp, n_dom = lax.axis_size("grp"), lax.axis_size("dom")
    line = n_dom // 2
    tiles = node_rows // TILE
    exports = boundary_cache.shape[0] // blk
    rows = hid_n // n_dom
    wide = hid_n + ch
    share = rows // n_grp
    links_wide = -(-(nb * slots + nb) // 128) * 128
    any_spec = pl.BlockSpec(memory_space=pl.ANY)
    vmem = pl.BlockSpec(memory_space=pltpu.VMEM)
    smem = pl.BlockSpec(memory_space=pltpu.SMEM)
    dma = pltpu.SemaphoreType.DMA
    V = pltpu.VMEM
    nodes = node_rows
    cost = pl.CostEstimate(
        flops=2 * nodes * hid_n * (7 * ch), bytes_accessed=8 * nodes * ch,
        transcendentals=nodes * hid_n,
    )
    out, gw = pl.pallas_call(
        functools.partial(layer_kernel, n_grp, n_dom),
        out_shape=(
            jax.ShapeDtypeStruct((nb, blk, ch), BF16),
            jax.ShapeDtypeStruct((n_grp, share, wide), BF16),
        ),
        in_specs=[smem] * 3 + [any_spec] * 6,
        out_specs=(any_spec,) * 2,
        scratch_shapes=[
            V((nb + (n_dom + 1) * exports, blk, ch), BF16),
            V(boundary_cache.shape, F32),
            V(adjacency.shape, BF16),
            V(weight_in.shape, BF16),
            V(weight_out.shape, BF16),
            V((tiles, TILE, ch), BF16),
            V((hid_n, 2 * ch), BF16),
            V((tiles, hid_n, TILE), F32),
            V((tiles, hid_n, TILE), F32),
            V((tiles, hid_n, TILE), BF16),
            V((tiles, hid_n, TILE), BF16),
            V((tiles, TILE, ch), BF16),
            V((line, hid_n, 2 * rows), F32),
            V((line, 2 * rows, ch), F32),
            V((nb, ch, blk), F32),
            V((nb * slots + 1, ch, blk), F32),
            V((nb, blk, ch), BF16),
            V((line, 2, rows, wide), F32),
            V((line, 2, rows, wide), BF16),
            V((line, rows, wide), BF16),
            V((line, n_grp, share, wide), F32),
            V((line, n_grp, share, wide), BF16),
            V((n_grp - 1, line, share, wide), BF16),
            V((line - 1, share, wide), BF16),
            V((line - 1, share, wide), BF16),
            V((n_grp, share, wide), BF16),
            V((8, links_wide), jnp.int32), pltpu.SMEM((8, links_wide), jnp.int32),
            dma((7,)), dma((2,)),
            dma((n_dom, exports, 3)), dma((n_dom, exports)),
            dma((line,)), dma((line,)),
            dma((n_grp - 1, line)), dma((n_grp - 1, line)),
            dma((line - 1,)), dma((line - 1,)),
            dma((n_grp - 1,)), dma((n_grp - 1,)),
        ],
        compiler_params=pltpu.CompilerParams(
            collective_id=0, has_side_effects=True, vmem_limit_bytes=56 * 2**20
        ),
        cost_estimate=cost,
    )(
        neighbor.T, counts, wanted, features.reshape(nb, blk, ch), boundary_cache, adjacency,
        weight_in, weight_out, cotangent.reshape(tiles, TILE, ch),
    )
    scale = 1.0 / math.sqrt(node_rows * n_grp * n_dom)
    out, gw_in, gw_out = pl.pallas_call(
        functools.partial(finish_kernel, scale),
        out_shape=(
            jax.ShapeDtypeStruct((node_rows, ch), BF16),
            jax.ShapeDtypeStruct((rows, hid_n), F32),
            jax.ShapeDtypeStruct((rows, ch), F32),
        ),
        in_specs=[any_spec, vmem],
        out_specs=(any_spec, vmem, vmem),
        scratch_shapes=[V((node_rows, ch), BF16), dma((4,)), dma((4,))],
        compiler_params=pltpu.CompilerParams(vmem_limit_bytes=56 * 2**20),
    )(out.reshape(node_rows, ch), gw.reshape(rows, wide))
    return out, gw_in, gw_out


def local(
    features, boundary_cache, adjacency, neighbor, counts, wanted, weight_in, weight_out, cotangent
):
    nblocks = adjacency.shape[0]
    slot_total = adjacency.shape[1]
    block_rows = adjacency.shape[2]
    channels = features.shape[1]
    node_rows = nblocks * block_rows
    partners = lax.axis_size("dom")
    cache_copy = boundary_cache.astype(jnp.bfloat16)
    exported = cache_copy.reshape(-1, block_rows, channels)
    export_total = exported.shape[0]
    exported_all = lax.all_gather(cache_copy, "dom", axis=0, tiled=True).reshape(
        partners, export_total, block_rows, channels
    )
    selected = wanted[0]
    boundary = exported_all[:, 0]
    boundary = jnp.where((selected == 1)[:, None, None], exported_all[:, 1], boundary)
    owned = features.reshape(nblocks, block_rows, channels)
    sources = jnp.concatenate([owned, boundary], 0)
    active = jnp.arange(slot_total)[None, :] < counts[:, None]
    chosen = sources[neighbor]
    chosen = jnp.where(active[:, :, None, None], chosen, jnp.zeros_like(chosen))
    aggregate = jnp.einsum("bsij,bsjf->bif", adjacency, chosen, preferred_element_type=jnp.float32)
    aggregate = aggregate.astype(jnp.bfloat16).reshape(node_rows, channels)
    joined = jnp.concatenate([aggregate, features], 1)
    preact = jnp.dot(joined, weight_in, preferred_element_type=jnp.float32)
    gating = jax.nn.sigmoid(preact)
    hidden = (preact * gating).astype(jnp.bfloat16)
    grad_hidden = jnp.einsum("nf,hf->nh", cotangent, weight_out, preferred_element_type=jnp.float32)
    grad_preact = (grad_hidden * gating * (1.0 + preact * (1.0 - gating))).astype(jnp.bfloat16)
    grad_joined = jnp.einsum(
        "nh,ch->nc", grad_preact, weight_in, preferred_element_type=jnp.float32
    )
    grad_aggregate = (
        grad_joined[:, :channels].astype(jnp.bfloat16).reshape(nblocks, block_rows, channels)
    )
    backward = jnp.einsum(
        "bsji,bjf->bsif", adjacency, grad_aggregate, preferred_element_type=jnp.float32
    )
    local_hit = active & (neighbor < nblocks)
    routing = (neighbor[None, :, :] == jnp.arange(nblocks)[:, None, None]) & local_hit[None]
    spread = jnp.einsum(
        "cbs,bsif->cif", routing.astype(jnp.float32), backward, precision=lax.Precision.HIGHEST
    )
    grad_features = (grad_joined[:, channels:] + spread.reshape(node_rows, channels)).astype(
        jnp.bfloat16
    )
    node_total = node_rows * lax.axis_size("grp") * partners
    loss_scale = 1.0 / math.sqrt(node_total)
    rows_in = weight_in.shape[0] // partners
    rows_out = weight_out.shape[0] // partners
    summed = lax.psum(
        (
            jnp.einsum("nc,nh->ch", joined, grad_preact, preferred_element_type=jnp.float32)
            * loss_scale,
            jnp.einsum("nh,nf->hf", hidden, cotangent, preferred_element_type=jnp.float32)
            * loss_scale,
        ),
        ("grp", "dom"),
    )
    position = lax.axis_index("dom")
    grad_weight_in = lax.dynamic_slice_in_dim(summed[0], position * rows_in, rows_in, 0)
    grad_weight_out = lax.dynamic_slice_in_dim(summed[1], position * rows_out, rows_out, 0)
    return (grad_features, grad_weight_in, grad_weight_out)


def solution(mesh):
    in_specs = (
        P(("grp", "dom"), None),
        P(("grp", "dom"), None),
        P(("grp", "dom"), None, None, None),
        P(("grp", "dom"), None),
        P(("grp", "dom")),
        P(("grp", "dom"), None),
        P(),
        P(),
        P(("grp", "dom"), None),
    )
    out_specs = (P(("grp", "dom"), None), P("dom", None), P("dom", None))
    n_grp, n_dom = mesh.shape["grp"], mesh.shape["dom"]

    def program(*args):
        rows = args[7].shape[0] // n_dom
        nodes = args[0].shape[0] // (n_grp * n_dom)
        fits = rows % (16 * n_grp) == 0 and (2 * rows) % 128 == 0 and nodes % TILE == 0
        body = fast_local if fits else local
        return sharded(body)(*args)

    def sharded(body):
        return jax.shard_map(
            body, mesh=mesh, in_specs=in_specs, out_specs=out_specs, check_vma=False
        )

    return program
```

```python
import functools
import math

import jax
import jax.numpy as jnp
from jax import lax
from jax.experimental import pallas as pl
from jax.experimental.pallas import tpu as pltpu
from jax.sharding import PartitionSpec as P

F32, BF16 = jnp.float32, jnp.bfloat16
TILE = 512
NT_DIMS = (((1,), (1,)), ((), ()))


def mm(a, b):
    return jnp.dot(a, b, preferred_element_type=F32)


def mm_nt(a, b):
    return lax.dot_general(a, b, NT_DIMS, preferred_element_type=F32)


def layer_kernel(
    n_grp, n_dom,
    nbr, cnt, wnt, feat_h, cache_h, adj_h, win_h, wout_h, cot_h,
    out_h, gw_h,
    src, cache, adj, win, wout, cot, win_t, pre2, gh, gps, hids, aggs, acc_in, acc_out,
    base, terms, out, own1, sb1, rb1, chip, sb2, rb2, sb3, rb3, gat4, table, links,
    load_sem, out_sem, b_send, b_recv, s1, r1, s2, r2, s3, r3, s4, r4,
):
    nb, slots, blk, _ = adj.shape
    exports = cache.shape[0] // blk
    line = n_dom // 2
    tiles = cot.shape[0]
    per = TILE // blk
    ch = cot.shape[2]
    hid_n = wout.shape[0]
    rows = rb1.shape[1]
    none = nb + n_dom * exports

    g = lax.axis_index("grp")
    d = lax.axis_index("dom")
    z, c = d // 2, lax.rem(d, 2)
    pair = z * 2 + (1 - c)

    def load(i, a, b):
        return pltpu.make_async_copy(a, b, load_sem.at[i])

    loads = [
        load(0, cache_h, cache),
        load(1, wout_h, wout),
        load(2, cot_h, cot),
        load(3, win_h, win),
        load(4, feat_h, src.at[pl.ds(0, nb)]),
        load(5, adj_h, adj),
    ]
    for item in loads:
        item.start()

    barrier = pltpu.get_barrier_semaphore()
    peers = [(g, pair)]
    peers += [(g, 2 * lax.rem(z + k, line) + c) for k in range(1, line)]
    peers += [(lax.rem(g + k, n_grp), d) for k in range(1, n_grp)]
    for peer in peers:
        pl.semaphore_signal(barrier, inc=1, device_id=peer, device_id_type=pl.DeviceIdType.MESH)

    loads[0].wait()
    src[pl.ds(nb + d * exports, exports)] = cache[...].astype(BF16).reshape(exports, blk, ch)
    pl.semaphore_wait(barrier, len(peers))

    def remote(a, b, send, recv, where):
        return pltpu.make_async_remote_copy(
            src_ref=a, dst_ref=b, send_sem=send, recv_sem=recv,
            device_id=where, device_id_type=pl.DeviceIdType.MESH,
        )

    def spread(q, e, way):
        part = src.at[nb + q * exports + e]
        to = (d + 2, d - 2, pair)[way]
        return remote(part, part, b_send.at[q, e, way], b_recv.at[q, e], (g, to))

    not_last, not_first = z < line - 1, z > 0
    for e in range(exports):
        pl.when(not_last)(lambda: spread(d, e, 0).start())
        pl.when(not_first)(lambda: spread(d, e, 1).start())
    for e in range(exports):
        spread(d, e, 2).start()

    pairs = nb * slots
    lane = lax.broadcasted_iota(jnp.int32, table.shape, 1)

    def target(b, s):
        return jnp.where(s < cnt[b], nbr[s, b], nb + n_dom)

    def ask(b, asked):
        for s in range(slots):
            asked = jnp.where(lane == b * slots + s, target(b, s), asked)
        return asked

    def find(b, found):
        for s in range(slots):
            p = b * slots + s
            hit = jnp.logical_and(asked == target(b, s), limit > p)
            found = jnp.where(hit, p + 1, found)
        return found

    limit = jnp.minimum(lane, pairs)
    asked = lax.fori_loop(0, nb, ask, lane - pairs)
    table[...] = lax.fori_loop(0, nb, find, jnp.zeros_like(lane))
    to_links = load(6, table, links)
    to_links.start()

    for item in loads[1:5]:
        item.wait()
    win_t[...] = win[...].astype(F32).T.astype(BF16)
    src[pl.ds(none, exports)] = jnp.zeros((exports, blk, ch), BF16)
    terms[0] = jnp.zeros((ch, blk), F32)

    def early(i, carry):
        gh[i] = mm_nt(wout[...], cot[i])
        own = src[pl.ds(i * per, per)].reshape(TILE, ch)
        pre2[i] = mm_nt(win_t[:, ch:], own)
        return carry

    done = 0
    for k in range(1, line):
        upto = tiles * k // (line - 1)
        lax.fori_loop(done, upto, early, 0)
        done = upto

        @pl.when(z - k >= 0)
        def _():
            for e in range(exports):
                spread(d - 2 * k, e, 0).wait_recv()
                pl.when(not_last)(lambda: spread(d - 2 * k, e, 0).start())
                spread(d - 2 * k, e, 2).start()

        @pl.when(z + k < line)
        def _():
            for e in range(exports):
                spread(d + 2 * k, e, 1).wait_recv()
                pl.when(not_first)(lambda: spread(d + 2 * k, e, 1).start())
                spread(d + 2 * k, e, 2).start()

    acc_in[...] = jnp.zeros_like(acc_in)
    acc_out[...] = jnp.zeros_like(acc_out)
    loads[5].wait()
    to_links.wait()
    for zz in range(line):
        for e in range(exports):
            spread(2 * zz + 1 - c, e, 2).wait_recv()

    def source(b, s):
        n = target(b, s)
        far = jnp.maximum(n - nb, 0)
        pick = wnt[0, jnp.minimum(far, n_dom - 1)]
        return src[jnp.where(n < nb, n, nb + far * exports + pick)]

    def front(i):
        parts = []
        for k in range(per):
            b = i * per + k
            left = jnp.concatenate([adj[b, s] for s in range(slots)], axis=1)
            right = jnp.concatenate([source(b, s) for s in range(slots)], axis=0)
            parts.append(mm(left, right).astype(BF16))
        agg = jnp.concatenate(parts, axis=0)
        pre = pre2[i] + mm_nt(win_t[:, :ch], agg)
        sg = 0.5 + 0.5 * jnp.tanh(0.5 * pre)
        h = pre * sg
        gps[i] = (gh[i] * (sg + h * (1.0 - sg))).astype(BF16)
        hids[i] = h.astype(BF16)
        aggs[i] = agg

    def weight_grads(i):
        gp = gps[i]
        own = src[pl.ds(i * per, per)].reshape(TILE, ch)
        for m, part in enumerate((aggs[i], own)):
            term = mm(gp, part)
            for j in range(ch // (2 * rows)):
                at = m * (ch // (2 * rows)) + j
                acc_in[at] += term[:, j * 2 * rows : (j + 1) * 2 * rows]
        acc_out[...] += mm(hids[i], cot[i]).reshape(acc_out.shape)

    def main(i, carry):
        weight_grads(i - 1)
        front(i)
        return carry

    front(0)
    lax.fori_loop(1, tiles, main, 0)
    weight_grads(tiles - 1)

    def late(i, carry):
        gj = mm(win[...], gps[i])
        gagg = gj[:ch].astype(BF16)
        for k in range(per):
            b = i * per + k
            cols = slice(k * blk, (k + 1) * blk)
            base[b] = gj[ch:, cols]
            both = mm(gagg[:, cols], jnp.concatenate([adj[b, s] for s in range(slots)], axis=1))
            for s in range(slots):
                terms[1 + b * slots + s] = both[:, s * blk : (s + 1) * blk]
        return carry

    def chain(b, carry):
        for s in range(slots):
            terms[1 + b * slots + s] += terms[links[0, b * slots + s]]
        return carry

    def write(b, carry):
        out[b] = (base[b] + terms[links[0, pairs + b]]).T.astype(BF16)
        return carry

    order = [lax.rem(z + k, line) for k in range(1, line + 1)]

    def step1(zz):
        return remote(sb1.at[zz, 1 - c], rb1.at[zz], s1.at[zz], r1.at[zz], (g, pair))

    for zz in order:
        whole = jnp.concatenate([acc_in[zz].T, acc_out[zz]], axis=1)
        whole = whole.reshape(2, rows, whole.shape[1])
        own1[zz] = whole
        sb1[zz] = whole.astype(BF16)
        step1(zz).start()
    lax.fori_loop(0, tiles // 3, late, 0)

    def step2(zz, k):
        to = lax.rem(g + k, n_grp)
        return remote(
            sb2.at[zz, to], rb2.at[k - 1, zz], s2.at[k - 1, zz], r2.at[k - 1, zz], (to, d)
        )

    for zz in order:
        step1(zz).wait_recv()
        both = (own1[zz, c] + rb1[zz].astype(F32)).reshape(chip.shape[1:])
        chip[zz] = both
        sb2[zz] = both.astype(BF16)
        for k in range(1, n_grp):
            step2(zz, k).start()

    lax.fori_loop(tiles // 3, tiles, late, 0)
    def step3(k):
        to = lax.rem(z + k, line)
        return remote(sb3.at[k - 1], rb3.at[k - 1], s3.at[k - 1], r3.at[k - 1], (g, 2 * to + c))

    total = None
    for k, zz in enumerate(order, 1):
        total = chip[zz, g]
        for j in range(1, n_grp):
            step2(zz, j).wait_recv()
            total += rb2[j - 1, zz].astype(F32)
        if k < line:
            sb3[k - 1] = total.astype(BF16)
            step3(k).start()
    lax.fori_loop(0, nb, chain, 0)
    for k in range(1, line):
        step3(k).wait_recv()
        total += rb3[k - 1].astype(F32)

    def step4(k):
        to = lax.rem(g + k, n_grp)
        return remote(gat4.at[g], gat4.at[g], s4.at[k - 1], r4.at[k - 1], (to, d))

    def arrive4(k):
        there = gat4.at[lax.rem(g - k + n_grp, n_grp)]
        return remote(there, there, s4.at[k - 1], r4.at[k - 1], (lax.rem(g + k, n_grp), d))

    gat4[g] = total.astype(BF16)
    for k in range(1, n_grp):
        step4(k).start()
    lax.fori_loop(0, nb, write, 0, unroll=4)
    store = pltpu.make_async_copy(out, out_h, out_sem.at[0])
    store.start()
    for k in range(1, n_grp):
        arrive4(k).wait_recv()
    last = pltpu.make_async_copy(gat4, gw_h, out_sem.at[1])
    last.start()

    for e in range(exports):
        pl.when(not_last)(lambda: spread(d, e, 0).wait_send())
        pl.when(not_first)(lambda: spread(d, e, 1).wait_send())
        spread(d, e, 2).wait_send()
    for k in range(1, line):

        @pl.when(z - k >= 0)
        def _():
            for e in range(exports):
                pl.when(not_last)(lambda: spread(d - 2 * k, e, 0).wait_send())
                spread(d - 2 * k, e, 2).wait_send()

        @pl.when(z + k < line)
        def _():
            for e in range(exports):
                pl.when(not_first)(lambda: spread(d + 2 * k, e, 1).wait_send())
                spread(d + 2 * k, e, 2).wait_send()

    for zz in order:
        step1(zz).wait_send()
        for k in range(1, n_grp):
            step2(zz, k).wait_send()
    for k in range(1, line):
        step3(k).wait_send()
    for k in range(1, n_grp):
        step4(k).wait_send()
    store.wait()
    last.wait()


def finish_kernel(scale, out_a, in_a, out_b, gw_in, gw_out, held, in_sems, out_sems):
    count = in_sems.shape[0]
    step = out_a.shape[0] // count
    parts = [pl.ds(i * step, step) for i in range(count)]
    loads = [
        pltpu.make_async_copy(out_a.at[p], held.at[p], in_sems.at[i]) for i, p in enumerate(parts)
    ]
    stores = [
        pltpu.make_async_copy(held.at[p], out_b.at[p], out_sems.at[i]) for i, p in enumerate(parts)
    ]
    for item in loads:
        item.start()
    value = in_a[...].astype(F32) * scale
    gw_in[...] = value[:, : gw_in.shape[1]]
    gw_out[...] = value[:, gw_in.shape[1] :]
    for load, store in zip(loads, stores):
        load.wait()
        store.start()
    for item in stores:
        item.wait()


def fast_local(
    features, boundary_cache, adjacency, neighbor, counts, wanted, weight_in, weight_out, cotangent
):
    nb, slots, blk, _ = adjacency.shape
    node_rows, ch = features.shape
    hid_n = weight_out.shape[0]
    n_grp, n_dom = lax.axis_size("grp"), lax.axis_size("dom")
    line = n_dom // 2
    tiles = node_rows // TILE
    exports = boundary_cache.shape[0] // blk
    rows = hid_n // n_dom
    wide = hid_n + ch
    share = rows // n_grp
    links_wide = -(-(nb * slots + nb) // 128) * 128
    any_spec = pl.BlockSpec(memory_space=pl.ANY)
    vmem = pl.BlockSpec(memory_space=pltpu.VMEM)
    smem = pl.BlockSpec(memory_space=pltpu.SMEM)
    dma = pltpu.SemaphoreType.DMA
    V = pltpu.VMEM
    nodes = node_rows
    cost = pl.CostEstimate(
        flops=2 * nodes * hid_n * (7 * ch), bytes_accessed=8 * nodes * ch,
        transcendentals=nodes * hid_n,
    )
    out, gw = pl.pallas_call(
        functools.partial(layer_kernel, n_grp, n_dom),
        out_shape=(
            jax.ShapeDtypeStruct((nb, blk, ch), BF16),
            jax.ShapeDtypeStruct((n_grp, share, wide), BF16),
        ),
        in_specs=[smem] * 3 + [any_spec] * 6,
        out_specs=(any_spec,) * 2,
        scratch_shapes=[
            V((nb + (n_dom + 1) * exports, blk, ch), BF16),
            V(boundary_cache.shape, F32),
            V(adjacency.shape, BF16),
            V(weight_in.shape, BF16),
            V(weight_out.shape, BF16),
            V((tiles, TILE, ch), BF16),
            V((hid_n, 2 * ch), BF16),
            V((tiles, hid_n, TILE), F32),
            V((tiles, hid_n, TILE), F32),
            V((tiles, hid_n, TILE), BF16),
            V((tiles, hid_n, TILE), BF16),
            V((tiles, TILE, ch), BF16),
            V((line, hid_n, 2 * rows), F32),
            V((line, 2 * rows, ch), F32),
            V((nb, ch, blk), F32),
            V((nb * slots + 1, ch, blk), F32),
            V((nb, blk, ch), BF16),
            V((line, 2, rows, wide), F32),
            V((line, 2, rows, wide), BF16),
            V((line, rows, wide), BF16),
            V((line, n_grp, share, wide), F32),
            V((line, n_grp, share, wide), BF16),
            V((n_grp - 1, line, share, wide), BF16),
            V((line - 1, share, wide), BF16),
            V((line - 1, share, wide), BF16),
            V((n_grp, share, wide), BF16),
            V((8, links_wide), jnp.int32), pltpu.SMEM((8, links_wide), jnp.int32),
            dma((7,)), dma((2,)),
            dma((n_dom, exports, 3)), dma((n_dom, exports)),
            dma((line,)), dma((line,)),
            dma((n_grp - 1, line)), dma((n_grp - 1, line)),
            dma((line - 1,)), dma((line - 1,)),
            dma((n_grp - 1,)), dma((n_grp - 1,)),
        ],
        compiler_params=pltpu.CompilerParams(
            collective_id=0, has_side_effects=True, vmem_limit_bytes=56 * 2**20
        ),
        cost_estimate=cost,
    )(
        neighbor.T, counts, wanted, features.reshape(nb, blk, ch), boundary_cache, adjacency,
        weight_in, weight_out, cotangent.reshape(tiles, TILE, ch),
    )
    scale = 1.0 / math.sqrt(node_rows * n_grp * n_dom)
    out, gw_in, gw_out = pl.pallas_call(
        functools.partial(finish_kernel, scale),
        out_shape=(
            jax.ShapeDtypeStruct((node_rows, ch), BF16),
            jax.ShapeDtypeStruct((rows, hid_n), F32),
            jax.ShapeDtypeStruct((rows, ch), F32),
        ),
        in_specs=[any_spec, vmem],
        out_specs=(any_spec, vmem, vmem),
        scratch_shapes=[V((node_rows, ch), BF16), dma((4,)), dma((4,))],
        compiler_params=pltpu.CompilerParams(vmem_limit_bytes=56 * 2**20),
    )(out.reshape(node_rows, ch), gw.reshape(rows, wide))
    return out, gw_in, gw_out


def local(
    features, boundary_cache, adjacency, neighbor, counts, wanted, weight_in, weight_out, cotangent
):
    nblocks = adjacency.shape[0]
    slot_total = adjacency.shape[1]
    block_rows = adjacency.shape[2]
    channels = features.shape[1]
    node_rows = nblocks * block_rows
    partners = lax.axis_size("dom")
    cache_copy = boundary_cache.astype(jnp.bfloat16)
    exported = cache_copy.reshape(-1, block_rows, channels)
    export_total = exported.shape[0]
    exported_all = lax.all_gather(cache_copy, "dom", axis=0, tiled=True).reshape(
        partners, export_total, block_rows, channels
    )
    selected = wanted[0]
    boundary = exported_all[:, 0]
    boundary = jnp.where((selected == 1)[:, None, None], exported_all[:, 1], boundary)
    owned = features.reshape(nblocks, block_rows, channels)
    sources = jnp.concatenate([owned, boundary], 0)
    active = jnp.arange(slot_total)[None, :] < counts[:, None]
    chosen = sources[neighbor]
    chosen = jnp.where(active[:, :, None, None], chosen, jnp.zeros_like(chosen))
    aggregate = jnp.einsum("bsij,bsjf->bif", adjacency, chosen, preferred_element_type=jnp.float32)
    aggregate = aggregate.astype(jnp.bfloat16).reshape(node_rows, channels)
    joined = jnp.concatenate([aggregate, features], 1)
    preact = jnp.dot(joined, weight_in, preferred_element_type=jnp.float32)
    gating = jax.nn.sigmoid(preact)
    hidden = (preact * gating).astype(jnp.bfloat16)
    grad_hidden = jnp.einsum("nf,hf->nh", cotangent, weight_out, preferred_element_type=jnp.float32)
    grad_preact = (grad_hidden * gating * (1.0 + preact * (1.0 - gating))).astype(jnp.bfloat16)
    grad_joined = jnp.einsum(
        "nh,ch->nc", grad_preact, weight_in, preferred_element_type=jnp.float32
    )
    grad_aggregate = (
        grad_joined[:, :channels].astype(jnp.bfloat16).reshape(nblocks, block_rows, channels)
    )
    backward = jnp.einsum(
        "bsji,bjf->bsif", adjacency, grad_aggregate, preferred_element_type=jnp.float32
    )
    local_hit = active & (neighbor < nblocks)
    routing = (neighbor[None, :, :] == jnp.arange(nblocks)[:, None, None]) & local_hit[None]
    spread = jnp.einsum(
        "cbs,bsif->cif", routing.astype(jnp.float32), backward, precision=lax.Precision.HIGHEST
    )
    grad_features = (grad_joined[:, channels:] + spread.reshape(node_rows, channels)).astype(
        jnp.bfloat16
    )
    node_total = node_rows * lax.axis_size("grp") * partners
    loss_scale = 1.0 / math.sqrt(node_total)
    rows_in = weight_in.shape[0] // partners
    rows_out = weight_out.shape[0] // partners
    summed = lax.psum(
        (
            jnp.einsum("nc,nh->ch", joined, grad_preact, preferred_element_type=jnp.float32)
            * loss_scale,
            jnp.einsum("nh,nf->hf", hidden, cotangent, preferred_element_type=jnp.float32)
            * loss_scale,
        ),
        ("grp", "dom"),
    )
    position = lax.axis_index("dom")
    grad_weight_in = lax.dynamic_slice_in_dim(summed[0], position * rows_in, rows_in, 0)
    grad_weight_out = lax.dynamic_slice_in_dim(summed[1], position * rows_out, rows_out, 0)
    return (grad_features, grad_weight_in, grad_weight_out)


def solution(mesh):
    in_specs = (
        P(("grp", "dom"), None),
        P(("grp", "dom"), None),
        P(("grp", "dom"), None, None, None),
        P(("grp", "dom"), None),
        P(("grp", "dom")),
        P(("grp", "dom"), None),
        P(),
        P(),
        P(("grp", "dom"), None),
    )
    out_specs = (P(("grp", "dom"), None), P("dom", None), P("dom", None))
    n_grp, n_dom = mesh.shape["grp"], mesh.shape["dom"]

    def program(*args):
        rows = args[7].shape[0] // n_dom
        nodes = args[0].shape[0] // (n_grp * n_dom)
        fits = rows % (16 * n_grp) == 0 and (2 * rows) % 128 == 0 and nodes % TILE == 0
        body = fast_local if fits else local
        return sharded(body)(*args)

    def sharded(body):
        return jax.shard_map(
            body, mesh=mesh, in_specs=in_specs, out_specs=out_specs, check_vma=False
        )

    return program
```

```python
import functools
import math

import jax
import jax.numpy as jnp
from jax import lax
from jax.experimental import pallas as pl
from jax.experimental.pallas import tpu as pltpu
from jax.sharding import PartitionSpec as P

F32, BF16 = jnp.float32, jnp.bfloat16
TILE = 512
NT_DIMS = (((1,), (1,)), ((), ()))


def mm(a, b):
    return jnp.dot(a, b, preferred_element_type=F32)


def mm_nt(a, b):
    return lax.dot_general(a, b, NT_DIMS, preferred_element_type=F32)


def layer_kernel(
    n_grp, n_dom,
    nbr, cnt, wnt, feat_h, cache_h, adj_h, win_h, wout_h, cot_h,
    out_h, gw_h,
    src, cache, adj, win, wout, cot, win_t, pre2, gh, gps, hids, aggs, acc_in, acc_out,
    base, terms, out, own1, sb1, rb1, chip, sb2, rb2, sb3, rb3, gat4, table, links,
    load_sem, out_sem, b_send, b_recv, s1, r1, s2, r2, s3, r3, s4, r4,
):
    nb, slots, blk, _ = adj.shape
    exports = cache.shape[0] // blk
    line = n_dom // 2
    tiles = cot.shape[0]
    per = TILE // blk
    ch = cot.shape[2]
    hid_n = wout.shape[0]
    rows = rb1.shape[1]
    none = nb + n_dom * exports

    g = lax.axis_index("grp")
    d = lax.axis_index("dom")
    z, c = d // 2, lax.rem(d, 2)
    pair = z * 2 + (1 - c)

    def load(i, a, b):
        return pltpu.make_async_copy(a, b, load_sem.at[i])

    loads = [
        load(0, cache_h, cache),
        load(1, wout_h, wout),
        load(2, cot_h, cot),
        load(3, win_h, win),
        load(4, feat_h, src.at[pl.ds(0, nb)]),
        load(5, adj_h, adj),
    ]
    for item in loads:
        item.start()

    barrier = pltpu.get_barrier_semaphore()
    peers = [(g, pair)]
    peers += [(g, 2 * lax.rem(z + k, line) + c) for k in range(1, line)]
    peers += [(lax.rem(g + k, n_grp), d) for k in range(1, n_grp)]
    for peer in peers:
        pl.semaphore_signal(barrier, inc=1, device_id=peer, device_id_type=pl.DeviceIdType.MESH)

    loads[0].wait()
    src[pl.ds(nb + d * exports, exports)] = cache[...].astype(BF16).reshape(exports, blk, ch)
    pl.semaphore_wait(barrier, len(peers))

    def remote(a, b, send, recv, where):
        return pltpu.make_async_remote_copy(
            src_ref=a, dst_ref=b, send_sem=send, recv_sem=recv,
            device_id=where, device_id_type=pl.DeviceIdType.MESH,
        )

    def spread(q, e, way):
        part = src.at[nb + q * exports + e]
        to = (d + 2, d - 2, pair)[way]
        return remote(part, part, b_send.at[q, e, way], b_recv.at[q, e], (g, to))

    not_last, not_first = z < line - 1, z > 0
    for e in range(exports):
        pl.when(not_last)(lambda: spread(d, e, 0).start())
        pl.when(not_first)(lambda: spread(d, e, 1).start())
    for e in range(exports):
        spread(d, e, 2).start()

    pairs = nb * slots
    lane = lax.broadcasted_iota(jnp.int32, table.shape, 1)

    def target(b, s):
        return jnp.where(s < cnt[b], nbr[s, b], nb + n_dom)

    def ask(b, asked):
        for s in range(slots):
            asked = jnp.where(lane == b * slots + s, target(b, s), asked)
        return asked

    def find(b, found):
        for s in range(slots):
            p = b * slots + s
            hit = jnp.logical_and(asked == target(b, s), limit > p)
            found = jnp.where(hit, p + 1, found)
        return found

    limit = jnp.minimum(lane, pairs)
    asked = lax.fori_loop(0, nb, ask, lane - pairs)
    table[...] = lax.fori_loop(0, nb, find, jnp.zeros_like(lane))
    to_links = load(6, table, links)
    to_links.start()

    for item in loads[1:5]:
        item.wait()
    win_t[...] = win[...].astype(F32).T.astype(BF16)
    src[pl.ds(none, exports)] = jnp.zeros((exports, blk, ch), BF16)
    terms[0] = jnp.zeros((ch, blk), F32)

    def early(i, carry):
        gh[i] = mm_nt(wout[...], cot[i])
        own = src[pl.ds(i * per, per)].reshape(TILE, ch)
        pre2[i] = mm_nt(win_t[:, ch:], own)
        return carry

    done = 0
    for k in range(1, line):
        upto = tiles * k // (line - 1)
        lax.fori_loop(done, upto, early, 0)
        done = upto

        @pl.when(z - k >= 0)
        def _():
            for e in range(exports):
                spread(d - 2 * k, e, 0).wait_recv()
                pl.when(not_last)(lambda: spread(d - 2 * k, e, 0).start())
                spread(d - 2 * k, e, 2).start()

        @pl.when(z + k < line)
        def _():
            for e in range(exports):
                spread(d + 2 * k, e, 1).wait_recv()
                pl.when(not_first)(lambda: spread(d + 2 * k, e, 1).start())
                spread(d + 2 * k, e, 2).start()

    acc_in[...] = jnp.zeros_like(acc_in)
    acc_out[...] = jnp.zeros_like(acc_out)
    loads[5].wait()
    to_links.wait()
    for zz in range(line):
        for e in range(exports):
            spread(2 * zz + 1 - c, e, 2).wait_recv()

    def source(b, s):
        n = target(b, s)
        far = jnp.maximum(n - nb, 0)
        pick = wnt[0, jnp.minimum(far, n_dom - 1)]
        return src[jnp.where(n < nb, n, nb + far * exports + pick)]

    def front(i):
        parts = []
        for k in range(per):
            b = i * per + k
            left = jnp.concatenate([adj[b, s] for s in range(slots)], axis=1)
            right = jnp.concatenate([source(b, s) for s in range(slots)], axis=0)
            parts.append(mm(left, right).astype(BF16))
        agg = jnp.concatenate(parts, axis=0)
        pre = pre2[i] + mm_nt(win_t[:, :ch], agg)
        sg = 0.5 + 0.5 * jnp.tanh(0.5 * pre)
        h = pre * sg
        gps[i] = (gh[i] * (sg + h * (1.0 - sg))).astype(BF16)
        hids[i] = h.astype(BF16)
        aggs[i] = agg

    def main(i, carry):
        front(i)
        return carry

    lax.fori_loop(0, tiles, main, 0)

    each = line // 2

    def weight_grads(half):
        def add(i, carry):
            part = src[pl.ds(i * per, per)].reshape(TILE, ch) if half else aggs[i]
            term = mm(gps[i], part)
            for j in range(each):
                acc_in[half * each + j] += term[:, j * 2 * rows : (j + 1) * 2 * rows]
            few = pl.ds(half * each * 2 * rows, each * 2 * rows)
            term = mm(hids[i, few], cot[i])
            acc_out[pl.ds(half * each, each)] += term.reshape(each, 2 * rows, ch)
            return carry

        lax.fori_loop(0, tiles, add, 0)

    def late(i, carry):
        gj = mm(win[...], gps[i])
        gagg = gj[:ch].astype(BF16)
        for k in range(per):
            b = i * per + k
            cols = slice(k * blk, (k + 1) * blk)
            base[b] = gj[ch:, cols]
            both = mm(gagg[:, cols], jnp.concatenate([adj[b, s] for s in range(slots)], axis=1))
            for s in range(slots):
                terms[1 + b * slots + s] = both[:, s * blk : (s + 1) * blk]
        return carry

    def chain(b, carry):
        for s in range(slots):
            terms[1 + b * slots + s] += terms[links[0, b * slots + s]]
        return carry

    def write(b, carry):
        out[b] = (base[b] + terms[links[0, pairs + b]]).T.astype(BF16)
        return carry

    order = [lax.rem(z + k, line) for k in range(1, line + 1)]

    def step1(zz):
        return remote(sb1.at[zz, 1 - c], rb1.at[zz], s1.at[zz], r1.at[zz], (g, pair))

    def send1(half):
        for zz in range(half * each, (half + 1) * each):
            whole = jnp.concatenate([acc_in[zz].T, acc_out[zz]], axis=1)
            whole = whole.reshape(2, rows, whole.shape[1])
            own1[zz] = whole
            sb1[zz] = whole.astype(BF16)
            step1(zz).start()

    def step2(zz, k):
        to = lax.rem(g + k, n_grp)
        return remote(
            sb2.at[zz, to], rb2.at[k - 1, zz], s2.at[k - 1, zz], r2.at[k - 1, zz], (to, d)
        )

    def send2(half):
        for zz in range(half * each, (half + 1) * each):
            step1(zz).wait_recv()
            both = (own1[zz, c] + rb1[zz].astype(F32)).reshape(chip.shape[1:])
            chip[zz] = both
            sb2[zz] = both.astype(BF16)
            for k in range(1, n_grp):
                step2(zz, k).start()

    weight_grads(0)
    send1(0)
    weight_grads(1)
    send2(0)
    send1(1)
    lax.fori_loop(0, tiles // 3, late, 0)
    send2(1)
    lax.fori_loop(tiles // 3, tiles, late, 0)
    def step3(k):
        to = lax.rem(z + k, line)
        return remote(sb3.at[k - 1], rb3.at[k - 1], s3.at[k - 1], r3.at[k - 1], (g, 2 * to + c))

    total = None
    for k, zz in enumerate(order, 1):
        total = chip[zz, g]
        for j in range(1, n_grp):
            step2(zz, j).wait_recv()
            total += rb2[j - 1, zz].astype(F32)
        if k < line:
            sb3[k - 1] = total.astype(BF16)
            step3(k).start()
    lax.fori_loop(0, nb, chain, 0)
    for k in range(1, line):
        step3(k).wait_recv()
        total += rb3[k - 1].astype(F32)

    def step4(k):
        to = lax.rem(g + k, n_grp)
        return remote(gat4.at[g], gat4.at[g], s4.at[k - 1], r4.at[k - 1], (to, d))

    def arrive4(k):
        there = gat4.at[lax.rem(g - k + n_grp, n_grp)]
        return remote(there, there, s4.at[k - 1], r4.at[k - 1], (lax.rem(g + k, n_grp), d))

    gat4[g] = total.astype(BF16)
    for k in range(1, n_grp):
        step4(k).start()
    lax.fori_loop(0, nb, write, 0, unroll=4)
    store = pltpu.make_async_copy(out, out_h, out_sem.at[0])
    store.start()
    for k in range(1, n_grp):
        arrive4(k).wait_recv()
    last = pltpu.make_async_copy(gat4, gw_h, out_sem.at[1])
    last.start()

    for e in range(exports):
        pl.when(not_last)(lambda: spread(d, e, 0).wait_send())
        pl.when(not_first)(lambda: spread(d, e, 1).wait_send())
        spread(d, e, 2).wait_send()
    for k in range(1, line):

        @pl.when(z - k >= 0)
        def _():
            for e in range(exports):
                pl.when(not_last)(lambda: spread(d - 2 * k, e, 0).wait_send())
                spread(d - 2 * k, e, 2).wait_send()

        @pl.when(z + k < line)
        def _():
            for e in range(exports):
                pl.when(not_first)(lambda: spread(d + 2 * k, e, 1).wait_send())
                spread(d + 2 * k, e, 2).wait_send()

    for zz in order:
        step1(zz).wait_send()
        for k in range(1, n_grp):
            step2(zz, k).wait_send()
    for k in range(1, line):
        step3(k).wait_send()
    for k in range(1, n_grp):
        step4(k).wait_send()
    store.wait()
    last.wait()


def finish_kernel(scale, out_a, in_a, out_b, gw_in, gw_out, held, in_sems, out_sems):
    count = in_sems.shape[0]
    step = out_a.shape[0] // count
    parts = [pl.ds(i * step, step) for i in range(count)]
    loads = [
        pltpu.make_async_copy(out_a.at[p], held.at[p], in_sems.at[i]) for i, p in enumerate(parts)
    ]
    stores = [
        pltpu.make_async_copy(held.at[p], out_b.at[p], out_sems.at[i]) for i, p in enumerate(parts)
    ]
    for item in loads:
        item.start()
    value = in_a[...].astype(F32) * scale
    gw_in[...] = value[:, : gw_in.shape[1]]
    gw_out[...] = value[:, gw_in.shape[1] :]
    for load, store in zip(loads, stores):
        load.wait()
        store.start()
    for item in stores:
        item.wait()


def fast_local(
    features, boundary_cache, adjacency, neighbor, counts, wanted, weight_in, weight_out, cotangent
):
    nb, slots, blk, _ = adjacency.shape
    node_rows, ch = features.shape
    hid_n = weight_out.shape[0]
    n_grp, n_dom = lax.axis_size("grp"), lax.axis_size("dom")
    line = n_dom // 2
    tiles = node_rows // TILE
    exports = boundary_cache.shape[0] // blk
    rows = hid_n // n_dom
    wide = hid_n + ch
    share = rows // n_grp
    links_wide = -(-(nb * slots + nb) // 128) * 128
    any_spec = pl.BlockSpec(memory_space=pl.ANY)
    vmem = pl.BlockSpec(memory_space=pltpu.VMEM)
    smem = pl.BlockSpec(memory_space=pltpu.SMEM)
    dma = pltpu.SemaphoreType.DMA
    V = pltpu.VMEM
    nodes = node_rows
    cost = pl.CostEstimate(
        flops=2 * nodes * hid_n * (7 * ch), bytes_accessed=8 * nodes * ch,
        transcendentals=nodes * hid_n,
    )
    out, gw = pl.pallas_call(
        functools.partial(layer_kernel, n_grp, n_dom),
        out_shape=(
            jax.ShapeDtypeStruct((nb, blk, ch), BF16),
            jax.ShapeDtypeStruct((n_grp, share, wide), BF16),
        ),
        in_specs=[smem] * 3 + [any_spec] * 6,
        out_specs=(any_spec,) * 2,
        scratch_shapes=[
            V((nb + (n_dom + 1) * exports, blk, ch), BF16),
            V(boundary_cache.shape, F32),
            V(adjacency.shape, BF16),
            V(weight_in.shape, BF16),
            V(weight_out.shape, BF16),
            V((tiles, TILE, ch), BF16),
            V((hid_n, 2 * ch), BF16),
            V((tiles, hid_n, TILE), F32),
            V((tiles, hid_n, TILE), F32),
            V((tiles, hid_n, TILE), BF16),
            V((tiles, hid_n, TILE), BF16),
            V((tiles, TILE, ch), BF16),
            V((line, hid_n, 2 * rows), F32),
            V((line, 2 * rows, ch), F32),
            V((nb, ch, blk), F32),
            V((nb * slots + 1, ch, blk), F32),
            V((nb, blk, ch), BF16),
            V((line, 2, rows, wide), F32),
            V((line, 2, rows, wide), BF16),
            V((line, rows, wide), BF16),
            V((line, n_grp, share, wide), F32),
            V((line, n_grp, share, wide), BF16),
            V((n_grp - 1, line, share, wide), BF16),
            V((line - 1, share, wide), BF16),
            V((line - 1, share, wide), BF16),
            V((n_grp, share, wide), BF16),
            V((8, links_wide), jnp.int32), pltpu.SMEM((8, links_wide), jnp.int32),
            dma((7,)), dma((2,)),
            dma((n_dom, exports, 3)), dma((n_dom, exports)),
            dma((line,)), dma((line,)),
            dma((n_grp - 1, line)), dma((n_grp - 1, line)),
            dma((line - 1,)), dma((line - 1,)),
            dma((n_grp - 1,)), dma((n_grp - 1,)),
        ],
        compiler_params=pltpu.CompilerParams(
            collective_id=0, has_side_effects=True, vmem_limit_bytes=56 * 2**20
        ),
        cost_estimate=cost,
    )(
        neighbor.T, counts, wanted, features.reshape(nb, blk, ch), boundary_cache, adjacency,
        weight_in, weight_out, cotangent.reshape(tiles, TILE, ch),
    )
    scale = 1.0 / math.sqrt(node_rows * n_grp * n_dom)
    out, gw_in, gw_out = pl.pallas_call(
        functools.partial(finish_kernel, scale),
        out_shape=(
            jax.ShapeDtypeStruct((node_rows, ch), BF16),
            jax.ShapeDtypeStruct((rows, hid_n), F32),
            jax.ShapeDtypeStruct((rows, ch), F32),
        ),
        in_specs=[any_spec, vmem],
        out_specs=(any_spec, vmem, vmem),
        scratch_shapes=[V((node_rows, ch), BF16), dma((4,)), dma((4,))],
        compiler_params=pltpu.CompilerParams(vmem_limit_bytes=56 * 2**20),
    )(out.reshape(node_rows, ch), gw.reshape(rows, wide))
    return out, gw_in, gw_out


def local(
    features, boundary_cache, adjacency, neighbor, counts, wanted, weight_in, weight_out, cotangent
):
    nblocks = adjacency.shape[0]
    slot_total = adjacency.shape[1]
    block_rows = adjacency.shape[2]
    channels = features.shape[1]
    node_rows = nblocks * block_rows
    partners = lax.axis_size("dom")
    cache_copy = boundary_cache.astype(jnp.bfloat16)
    exported = cache_copy.reshape(-1, block_rows, channels)
    export_total = exported.shape[0]
    exported_all = lax.all_gather(cache_copy, "dom", axis=0, tiled=True).reshape(
        partners, export_total, block_rows, channels
    )
    selected = wanted[0]
    boundary = exported_all[:, 0]
    boundary = jnp.where((selected == 1)[:, None, None], exported_all[:, 1], boundary)
    owned = features.reshape(nblocks, block_rows, channels)
    sources = jnp.concatenate([owned, boundary], 0)
    active = jnp.arange(slot_total)[None, :] < counts[:, None]
    chosen = sources[neighbor]
    chosen = jnp.where(active[:, :, None, None], chosen, jnp.zeros_like(chosen))
    aggregate = jnp.einsum("bsij,bsjf->bif", adjacency, chosen, preferred_element_type=jnp.float32)
    aggregate = aggregate.astype(jnp.bfloat16).reshape(node_rows, channels)
    joined = jnp.concatenate([aggregate, features], 1)
    preact = jnp.dot(joined, weight_in, preferred_element_type=jnp.float32)
    gating = jax.nn.sigmoid(preact)
    hidden = (preact * gating).astype(jnp.bfloat16)
    grad_hidden = jnp.einsum("nf,hf->nh", cotangent, weight_out, preferred_element_type=jnp.float32)
    grad_preact = (grad_hidden * gating * (1.0 + preact * (1.0 - gating))).astype(jnp.bfloat16)
    grad_joined = jnp.einsum(
        "nh,ch->nc", grad_preact, weight_in, preferred_element_type=jnp.float32
    )
    grad_aggregate = (
        grad_joined[:, :channels].astype(jnp.bfloat16).reshape(nblocks, block_rows, channels)
    )
    backward = jnp.einsum(
        "bsji,bjf->bsif", adjacency, grad_aggregate, preferred_element_type=jnp.float32
    )
    local_hit = active & (neighbor < nblocks)
    routing = (neighbor[None, :, :] == jnp.arange(nblocks)[:, None, None]) & local_hit[None]
    spread = jnp.einsum(
        "cbs,bsif->cif", routing.astype(jnp.float32), backward, precision=lax.Precision.HIGHEST
    )
    grad_features = (grad_joined[:, channels:] + spread.reshape(node_rows, channels)).astype(
        jnp.bfloat16
    )
    node_total = node_rows * lax.axis_size("grp") * partners
    loss_scale = 1.0 / math.sqrt(node_total)
    rows_in = weight_in.shape[0] // partners
    rows_out = weight_out.shape[0] // partners
    summed = lax.psum(
        (
            jnp.einsum("nc,nh->ch", joined, grad_preact, preferred_element_type=jnp.float32)
            * loss_scale,
            jnp.einsum("nh,nf->hf", hidden, cotangent, preferred_element_type=jnp.float32)
            * loss_scale,
        ),
        ("grp", "dom"),
    )
    position = lax.axis_index("dom")
    grad_weight_in = lax.dynamic_slice_in_dim(summed[0], position * rows_in, rows_in, 0)
    grad_weight_out = lax.dynamic_slice_in_dim(summed[1], position * rows_out, rows_out, 0)
    return (grad_features, grad_weight_in, grad_weight_out)


def solution(mesh):
    in_specs = (
        P(("grp", "dom"), None),
        P(("grp", "dom"), None),
        P(("grp", "dom"), None, None, None),
        P(("grp", "dom"), None),
        P(("grp", "dom")),
        P(("grp", "dom"), None),
        P(),
        P(),
        P(("grp", "dom"), None),
    )
    out_specs = (P(("grp", "dom"), None), P("dom", None), P("dom", None))
    n_grp, n_dom = mesh.shape["grp"], mesh.shape["dom"]

    def program(*args):
        rows = args[7].shape[0] // n_dom
        nodes = args[0].shape[0] // (n_grp * n_dom)
        fits = args[7].shape[0] == 2 * args[0].shape[1] and n_dom % 4 == 0
        fits = fits and rows % (16 * n_grp) == 0 and (2 * rows) % 128 == 0 and nodes % TILE == 0
        body = fast_local if fits else local
        return sharded(body)(*args)

    def sharded(body):
        return jax.shard_map(
            body, mesh=mesh, in_specs=in_specs, out_specs=out_specs, check_vma=False
        )

    return program
```
